256 devices in a mesh: dp: 16 (over z, core), tensor: 16 (over x, y).
Axes of the slice: x: 4, y: 4, z: 8, core: 2. Of those that a mesh axis runs over, the one named last changes fastest.
Arguments:
- qkv_img: bfloat16 [16, 1024, 3, 2432], P('dp', 'tensor'), may hold values from -16 to 16
- tan_img: bfloat16 [16, 1024, 3, 2432], P('dp', 'tensor'), may hold values from -96 to 96
- txt_kv: bfloat16 [16, 48, 333, 256], P('dp', 'tensor'), may hold values from -5 to 5
- head_table: int32 [16, 3], replicated, may hold values from -1 to 37, as said below
- out_weight: bfloat16 [3072, 2432], P('tensor'), may hold values from -2.390625 to 2.390625
- cotangent: bfloat16 [16, 1024, 2432], P('dp', 'tensor'), may hold values from -6 to 6
Outputs:
- image_out: bfloat16 [16, 1024, 2432], P('dp', 'tensor')
- tangent_out: bfloat16 [16, 1024, 2432], P('dp', 'tensor')
- weight_grad: float32 [3072, 2432], P('tensor')
The draws below stay inside these ranges and needn't reach their ends.
Inputs may be any that keep to these rules, and one draw needn't show every extreme that they name: `head_table`: each of the 38 heads stands in exactly one slot and the other slots hold -1; some index of tensor has all 3 slots filled.
All inputs are finite; a program needn't handle non-finite values.
Results may differ from the reference program's by a relative error of at most 0.023.
Values may be sent and summed in bfloat16 or wider, within the bound.
A program may use at most 128 MiB of HBM per device.

```python
import math
import jax
import jax.numpy as jnp
from jax import lax

HEADS = 38
HD = 64
D = 2432
TXT = 333
IMG = 1024
SLOTS = 3
SAMPLES = 16
N_TENSOR = 16


def draw_qkv_img(key, part):
    key = jax.random.fold_in(key, 11)
    first_key = jax.random.fold_in(key, 0)
    shape = (SAMPLES, IMG, 3, D)
    return jnp.clip(jax.random.normal(first_key, shape, jnp.float32), -4.0, 4.0).astype(jnp.bfloat16)


def draw_tan_img(key, part):
    key = jax.random.fold_in(key, 23)
    first_key = jax.random.fold_in(key, 0)
    second_key = jax.random.fold_in(key, 1)
    fourth_key = jax.random.fold_in(key, 3)
    shape = (SAMPLES, IMG, 3, D)
    positions = jnp.arange(IMG).astype(jnp.float32)
    base = jnp.clip(jax.random.normal(first_key, shape, jnp.float32), -4.0, 4.0)
    trend = 3.0 ** (positions / IMG)
    half_decade = 0.5 * math.log(10.0)
    row_scale = jnp.exp(half_decade * jax.random.uniform(second_key, (SAMPLES, IMG, 1, 1), jnp.float32))
    column_scale = jnp.exp(half_decade * jax.random.uniform(fourth_key, (1, 1, 1, D), jnp.float32))
    return (base * trend[None, :, None, None] * row_scale * column_scale / 3.0).astype(jnp.bfloat16)


def draw_head_table(key, part):
    key = jax.random.fold_in(key, 5)
    order = jax.random.permutation(key, N_TENSOR * SLOTS)
    table = jnp.where(order < HEADS, order, -1)
    return table.reshape(N_TENSOR, SLOTS).astype(jnp.int32)


def levels(stream_key, dims, pieces, smallest, top_value):
    def one(axis_at, parts):
        heights = jax.random.uniform(jax.random.fold_in(jax.random.fold_in(stream_key, 6), axis_at), (parts,), jnp.float32, smallest / len(pieces), top_value / len(pieces))
        return jnp.repeat(jnp.exp(heights), dims[axis_at] // parts).reshape((-1,) + (1,) * (len(dims) - axis_at - 1))

    loudness = one(*pieces[0])
    for cut in pieces[1:]:
        loudness = loudness * one(*cut)
    return loudness


def noise(rng, dims, spread, reach, cuts=(), dtype=jnp.bfloat16):
    array = spread * jax.random.normal(rng, dims, jnp.float32)
    if cuts:
        array = array * levels(rng, dims, cuts, -0.22, 0.18)
    return jnp.clip(array, -reach, reach).astype(dtype)


def setup_inputs(seed: int = 0) -> dict:
    key_list = jax.random.split(jax.random.key(seed), 7)
    return {
        "qkv_img": draw_qkv_img(jax.random.fold_in(key_list[6], 71), 0),
        "tan_img": draw_tan_img(jax.random.fold_in(key_list[6], 71), 0),
        "txt_kv": noise(key_list[2], (SAMPLES, N_TENSOR * SLOTS, TXT, 4 * HD), 1.0, 5.0, ((0, 16), (1, 16))),
        "head_table": draw_head_table(jax.random.fold_in(key_list[6], 71), 0),
        "out_weight": noise(key_list[4], (N_TENSOR * SLOTS * HD, D), 0.4, 2.390625, ((0, 16),)),
        "cotangent": noise(key_list[5], (SAMPLES, IMG, D), 1.0, 6.0, ((0, 16), (1, 16))),
    }


def attend(slot_data, text_rows, filled):
    head_size = text_rows.shape[1] // 4
    score_scale = head_size ** (-0.5)
    queries = slot_data[:, :head_size]
    tangent_queries = slot_data[:, 3 * head_size:4 * head_size]
    key_rows = jnp.concatenate([slot_data[:, head_size:2 * head_size], text_rows[:, :head_size]], 0)
    value_rows = jnp.concatenate([slot_data[:, 2 * head_size:3 * head_size], text_rows[:, head_size:2 * head_size]], 0)
    tangent_keys = jnp.concatenate([slot_data[:, 4 * head_size:5 * head_size], text_rows[:, 2 * head_size:3 * head_size]], 0)
    tangent_values = jnp.concatenate([slot_data[:, 5 * head_size:], text_rows[:, 3 * head_size:]], 0)
    scores = jnp.dot(queries, key_rows.T, preferred_element_type=jnp.float32) * score_scale
    tangent_scores = (jnp.dot(tangent_queries, key_rows.T, preferred_element_type=jnp.float32) + jnp.dot(queries, tangent_keys.T, preferred_element_type=jnp.float32)) * score_scale
    row_max = lax.optimization_barrier(jnp.max(scores, axis=1, keepdims=True))
    expanded = jnp.exp(scores - row_max)
    probs = expanded / lax.optimization_barrier(jnp.sum(expanded, axis=1, keepdims=True))
    tangent_probs = probs * (tangent_scores - lax.optimization_barrier(jnp.sum(probs * tangent_scores, axis=1, keepdims=True)))
    probs_low = probs.astype(jnp.bfloat16)
    tangent_low = tangent_probs.astype(jnp.bfloat16)
    attn_out = jnp.dot(probs_low, value_rows, preferred_element_type=jnp.float32)
    attn_tan = jnp.dot(tangent_low, value_rows, preferred_element_type=jnp.float32) + jnp.dot(probs_low, tangent_values, preferred_element_type=jnp.float32)
    joined = jnp.concatenate([attn_out, attn_tan], 1)
    return jnp.where(filled, joined, jnp.zeros_like(joined)).astype(jnp.bfloat16)

def reference(qkv_img, tan_img, txt_kv, head_table, out_weight, cotangent):
    flat_table = head_table.reshape(-1)
    head_ids = jnp.maximum(flat_table, 0).astype(jnp.int32)
    filled = flat_table >= 0
    weight_slots = out_weight.reshape(N_TENSOR * SLOTS, HD, D).astype(jnp.float32)

    def one_sample(running, inputs):
        sample_qkv, sample_tan, sample_text, sample_cot = inputs
        stacked = jnp.concatenate([sample_qkv, sample_tan], 1).reshape(IMG, 6, HEADS, HD)

        def one_slot(slot_inputs):
            head_id, slot_filled, text_rows = slot_inputs
            slot_data = lax.dynamic_index_in_dim(stacked, head_id, 2, keepdims=False).reshape(IMG, 6 * HD)
            return attend(slot_data, text_rows, slot_filled)
        per_slot = lax.map(one_slot, (head_ids, filled, sample_text))
        attn_out = per_slot[:, :, :HD].astype(jnp.float32)
        attn_tan = per_slot[:, :, HD:].astype(jnp.float32)
        proj_sum = jnp.einsum('ric,rcd->id', attn_out, weight_slots)
        tan_sum = jnp.einsum('ric,rcd->id', attn_tan, weight_slots)
        image_out = proj_sum.astype(jnp.bfloat16)
        root_mean = jnp.sqrt(jnp.sum(tan_sum * tan_sum) / (IMG * D))
        tangent_out = (tan_sum / (root_mean + 0.1)).astype(jnp.bfloat16)
        upstream = (sample_cot.astype(jnp.float32) - tangent_out.astype(jnp.float32)).astype(jnp.bfloat16)
        grad_term = jnp.einsum('ric,id->rcd', attn_out, upstream.astype(jnp.float32))
        return (running + grad_term, (image_out, tangent_out))
    initial = jnp.zeros((N_TENSOR * SLOTS, HD, D), jnp.float32)
    summed, (image_out, tangent_out) = lax.scan(one_sample, initial, (qkv_img, tan_img, txt_kv, cotangent))
    weight_grad = (summed / SAMPLES).reshape(N_TENSOR * SLOTS * HD, D)
    return (image_out, tangent_out, weight_grad)
```

```python
import functools

import jax
import jax.numpy as jnp
from jax import lax
from jax.experimental import pallas as pl
from jax.experimental.pallas import tpu as pltpu
from jax.sharding import PartitionSpec as P

MESH = pl.DeviceIdType.MESH
F32 = jnp.float32
LOW = jnp.bfloat16


def swap_halves(value):
    return pltpu.roll(value, 64, 1)


def pack(n_t, slots, table, qkv, tan, outbox, live):
    low_half = lax.broadcasted_iota(jnp.int32, (1, 128), 1) < 64

    def one_device(t, carry):
        for s in range(slots):
            entry = table[t * slots + s]
            head = jnp.maximum(entry, 0)
            span = pl.ds(pl.multiple_of((head // 2) * 128, 128), 128)
            odd = jnp.full((1, 128), head % 2, jnp.int32) == 1
            live[s, t] = jnp.where(jnp.full((8, 128), entry, jnp.int32) >= 0, 1.0, 0.0)

            def pair(a, b, odd=odd):
                a = a.astype(F32)
                b = b.astype(F32)
                first = jnp.where(odd, swap_halves(a), a)
                second = jnp.where(odd, b, swap_halves(b))
                return jnp.where(low_half, first, second)

            outbox[s, t, :, 0:128] = (pair(tan[0, :, span], qkv[0, :, span]) * 0.125).astype(LOW)
            outbox[s, t, :, 128:256] = pair(qkv[1, :, span], tan[1, :, span]).astype(LOW)
            outbox[s, t, :, 256:384] = pair(qkv[2, :, span], tan[2, :, span]).astype(LOW)
        return carry

    lax.fori_loop(0, n_t, one_device, 0)


def body(
    dims,
    outbox,
    live,
    txt,
    weight,
    cot,
    image_out,
    tangent_out,
    grad_out,
    arrived,
    text_pad,
    score_rhs,
    value_rhs,
    attn,
    regroup,
    group_weight,
    proj_lhs,
    prim_t,
    part_out,
    part_in,
    tan_sum,
    squares,
    upstream,
    up_all,
    twin_out,
    twin_in,
    grad_send,
    grad_in,
    z_out,
    z_in,
    final,
    a_send,
    a_recv,
    w_send,
    w_recv,
    f_send,
    f_recv,
    own_sem,
    p_send,
    p_recv,
    r_send,
    r_recv,
    q_send,
    q_recv,
    u_send,
    u_recv,
    t_send,
    t_recv,
    g_send,
    g_recv,
    z_send,
    z_recv,
    c_send,
    c_recv,
    s_send,
    s_recv,
):
    n_t, side, n_z, slots, rows, keys, keys_pad, half, offset, width, txt_len = dims
    me = lax.axis_index("tensor")
    dp = lax.axis_index("dp")
    x = me // side
    y = me % side
    z = dp // 2
    c = dp % 2
    img = n_t * rows
    group_rows = side * rows

    def line(o, k):
        return (1 - o) * (x * side + k) + o * (k * side + y)

    def place(o):
        return (1 - o) * y + o * x

    def twin():
        return {"dp": z * 2 + (1 - c)}

    low_half = lax.broadcasted_iota(jnp.int32, (1, 128), 1) < 64

    for o in range(2):
        for k in range(side):
            group_weight[o, k * 256 + 192 : k * 256 + 256, :] = jnp.zeros((64, half), LOW)

    barrier = pltpu.get_barrier_semaphore()

    def greet(i, carry):
        t = ((x + i // side) % side) * side + (y + i % side) % side
        pl.semaphore_signal(barrier, inc=1, device_id={"tensor": t}, device_id_type=MESH)
        return carry

    lax.fori_loop(1, n_t, greet, 0)

    def greet_z(i, carry):
        pl.semaphore_signal(
            barrier, inc=1, device_id={"dp": ((z + i) % n_z) * 2 + c}, device_id_type=MESH
        )
        return carry

    lax.fori_loop(1, n_z, greet_z, 0)
    pl.semaphore_signal(barrier, inc=1, device_id=twin(), device_id_type=MESH)
    pl.semaphore_wait(barrier, n_t + n_z - 1)

    def in_copy(s, t):
        return pltpu.make_async_remote_copy(
            src_ref=outbox.at[s, t],
            dst_ref=arrived.at[s, me],
            send_sem=a_send.at[s, t],
            recv_sem=a_recv.at[s, me],
            device_id={"tensor": t},
            device_id_type=MESH,
        )

    def send_slot(s, carry):
        def send_one(i, inner):
            t = ((x + i // side) % side) * side + (y + i % side) % side
            in_copy(s, t).start()
            return inner

        lax.fori_loop(1, n_t, send_one, 0)
        pltpu.make_async_copy(outbox.at[s, me], arrived.at[s, me], own_sem.at[1 + s]).start()
        return carry

    lax.fori_loop(0, slots, send_slot, 0)

    half_at = pl.multiple_of(c * offset, 128)

    def w_copy(k):
        return pltpu.make_async_remote_copy(
            src_ref=weight.at[:, pl.ds(half_at, half)],
            dst_ref=group_weight.at[c, pl.ds(place(c) * 256, 192)],
            send_sem=w_send.at[k],
            recv_sem=w_recv.at[place(c)],
            device_id={"tensor": line(c, k)},
            device_id_type=MESH,
        )

    def w_own():
        return pltpu.make_async_copy(
            weight.at[:, pl.ds(half_at, half)],
            group_weight.at[c, pl.ds(place(c) * 256, 192)],
            own_sem.at[0],
        )

    def f_copy(k):
        return pltpu.make_async_remote_copy(
            src_ref=group_weight.at[c, pl.ds(k * 256, 192)],
            dst_ref=group_weight.at[c, pl.ds(k * 256, 192)],
            send_sem=f_send.at[k],
            recv_sem=f_recv.at[k],
            device_id=twin(),
            device_id_type=MESH,
        )

    def f_arrival(k):
        return pltpu.make_async_remote_copy(
            src_ref=group_weight.at[1 - c, pl.ds(k * 256, 192)],
            dst_ref=group_weight.at[1 - c, pl.ds(k * 256, 192)],
            send_sem=f_send.at[k],
            recv_sem=f_recv.at[k],
            device_id=twin(),
            device_id_type=MESH,
        )

    w_own().start()
    for i in range(1, side):
        w_copy((place(c) + i) % side).start()

    for s in range(slots):
        text_pad[320:384, :] = jnp.zeros((64, 256), LOW)
        text_pad[0:txt_len, :] = txt[s]
        kv = text_pad[:, 0:128].astype(F32)
        dkv = text_pad[:, 128:256].astype(F32)
        key_pair = jnp.where(low_half, kv, swap_halves(dkv))
        val_pair = jnp.where(low_half, swap_halves(kv), dkv)
        key_t = key_pair.T.astype(LOW)
        score_rhs[s, 0:64, 0:keys_pad] = jnp.zeros((64, keys_pad), LOW)
        score_rhs[s, 64:128, img:keys_pad] = key_t[0:64]
        score_rhs[s, :, keys_pad + img : 2 * keys_pad] = key_t
        value_rhs[s, img:keys_pad, :] = val_pair.astype(LOW)
        value_rhs[s, keys_pad + img : 2 * keys_pad, :] = jnp.where(low_half, 0.0, kv).astype(LOW)

    def p_copy(s, o, k):
        source = attn.at[s, :, k] if o == 0 else attn.at[s, k]
        return pltpu.make_async_remote_copy(
            src_ref=source,
            dst_ref=regroup.at[o, s, place(o)],
            send_sem=p_send.at[o, s, k],
            recv_sem=p_recv.at[o, s, place(o)],
            device_id={"tensor": line(o, k)},
            device_id_type=MESH,
        )

    def one_slot(s, carry):
        def arrival(i, inner):
            t = (me + i) % n_t
            pltpu.make_async_remote_copy(
                src_ref=outbox.at[s, t],
                dst_ref=arrived.at[s, t],
                send_sem=a_send.at[s, t],
                recv_sem=a_recv.at[s, t],
                device_id={"tensor": t},
                device_id_type=MESH,
            ).wait_recv()
            return inner

        lax.fori_loop(1, n_t, arrival, 0)
        pltpu.make_async_copy(outbox.at[s, me], arrived.at[s, me], own_sem.at[1 + s]).wait()
        key_t = arrived[s, :, :, 128:256].reshape(img, 128).astype(F32).T.astype(LOW)
        score_rhs[s, 64:128, 0:img] = key_t[0:64]
        score_rhs[s, :, keys_pad : keys_pad + img] = key_t
        val_pair = arrived[s, :, :, 256:384].reshape(img, 128)
        value_rhs[s, 0:img, :] = val_pair
        value_rhs[s, keys_pad : keys_pad + img, :] = jnp.where(
            low_half, 0.0, swap_halves(val_pair.astype(F32))
        ).astype(LOW)
        filled = live[s, me, 0:1, :]

        def one_block(q, inner):
            lhs = arrived[s, pl.ds(q * side, side), :, 0:128].reshape(group_rows, 128)
            scores = jnp.dot(lhs, score_rhs[s, :, 0:keys_pad], preferred_element_type=F32)
            tangents = jnp.dot(
                lhs, score_rhs[s, :, keys_pad : 2 * keys_pad], preferred_element_type=F32
            )
            valid = lax.broadcasted_iota(jnp.int32, (1, 128), 1) < keys - (keys_pad - 128)
            scores = jnp.concatenate(
                [
                    scores[:, : keys_pad - 128],
                    jnp.where(valid, scores[:, keys_pad - 128 :], -1e30),
                ],
                1,
            )
            top = jnp.max(scores, axis=1, keepdims=True)
            raised = jnp.exp(scores - top)
            total = jnp.sum(raised, axis=1, keepdims=True)
            mean = jnp.sum(raised * tangents, axis=1, keepdims=True) / total
            shifted = raised * (tangents - mean)
            joined = jnp.dot(
                raised.astype(LOW), value_rhs[s, 0:keys_pad, :], preferred_element_type=F32
            ) + jnp.dot(
                shifted.astype(LOW),
                value_rhs[s, keys_pad : 2 * keys_pad, :],
                preferred_element_type=F32,
            )
            joined = (joined / total * filled).astype(LOW)
            attn[s, q] = joined.reshape(side, rows, 128)
            return inner

        lax.fori_loop(0, side, one_block, 0)
        for o in range(2):
            own = place(o)
            for i in range(1, side):
                p_copy(s, o, (own + i) % side).start()
        regroup[0, s, y] = attn[s, :, y]
        regroup[1, s, x] = attn[s, x]

        @pl.when(s == slots - 2)
        def _():
            w_own().wait()
            for i in range(1, side):
                k = (place(c) + i) % side
                pltpu.make_async_remote_copy(
                    src_ref=weight.at[:, pl.ds(half_at, half)],
                    dst_ref=group_weight.at[c, pl.ds(k * 256, 192)],
                    send_sem=w_send.at[k],
                    recv_sem=w_recv.at[k],
                    device_id={"tensor": line(c, k)},
                    device_id_type=MESH,
                ).wait_recv()
            for k in range(side):
                f_copy(k).start()

        return carry

    lax.fori_loop(0, slots, one_slot, 0)

    def r_copy(o, j, k):
        span = pl.ds(pl.multiple_of(j * (half // 2), 128), half // 2)
        return pltpu.make_async_remote_copy(
            src_ref=part_out.at[o, k, :, :, span],
            dst_ref=part_in.at[o, place(1 - o), :, :, span],
            send_sem=r_send.at[o, j, k],
            recv_sem=r_recv.at[o, j, place(1 - o)],
            device_id={"tensor": line(1 - o, k)},
            device_id_type=MESH,
        )

    for k in range(side):
        f_arrival(k).wait_recv()

    for o in range(2):
        for s in range(slots):
            for i in range(1, side):
                k = (place(o) + i) % side
                pltpu.make_async_remote_copy(
                    src_ref=regroup.at[o, s, k],
                    dst_ref=regroup.at[o, s, k],
                    send_sem=p_send.at[o, s, k],
                    recv_sem=p_recv.at[o, s, k],
                    device_id={"tensor": line(o, k)},
                    device_id_type=MESH,
                ).wait_recv()

        def arrange(k, carry, o=o):
            first = regroup[o, 0, k].reshape(group_rows, 128).astype(F32)
            second = regroup[o, 1, k].reshape(group_rows, 128).astype(F32)
            third = regroup[o, 2, k].reshape(group_rows, 128).astype(F32)
            prim = jnp.where(low_half, first, swap_halves(second))
            prim_last = jnp.where(low_half, third, 0.0)
            tang = jnp.where(low_half, swap_halves(first), second)
            tang_last = jnp.where(low_half, swap_halves(third), 0.0)
            at = pl.multiple_of(k * 256, 256)
            proj_lhs[o, 0:group_rows, pl.ds(at, 128)] = prim.astype(LOW)
            proj_lhs[o, 0:group_rows, pl.ds(at + 128, 128)] = prim_last.astype(LOW)
            proj_lhs[o, group_rows : 2 * group_rows, pl.ds(at, 128)] = tang.astype(LOW)
            proj_lhs[o, group_rows : 2 * group_rows, pl.ds(at + 128, 128)] = tang_last.astype(LOW)
            prim_t[o, k, 0:128, :] = prim.T.astype(LOW)
            prim_t[o, k, 128:192, :] = prim_last.T[0:64].astype(LOW)
            return carry

        lax.fori_loop(0, side, arrange, 0)

        def project(j, carry, o=o):
            span = pl.ds(pl.multiple_of(j * (half // 2), 128), half // 2)
            part = jnp.dot(
                proj_lhs[o], group_weight[o, :, span], preferred_element_type=F32
            ).astype(LOW)
            for k in range(side):
                for kind in range(2):
                    at = kind * group_rows + k * rows
                    part_out[o, k, kind, :, span] = part[at : at + rows]
            own = place(1 - o)
            for i in range(1, side):
                r_copy(o, j, (own + i) % side).start()
            part_in[o, own, :, :, span] = part_out[o, own, :, :, span]
            return carry

        lax.fori_loop(0, 2, project, 0)

    for o in range(2):
        for j in range(2):
            for i in range(1, side):
                k = (place(1 - o) + i) % side
                span = pl.ds(j * (half // 2), half // 2)
                pltpu.make_async_remote_copy(
                    src_ref=part_out.at[o, k, :, :, span],
                    dst_ref=part_in.at[o, k, :, :, span],
                    send_sem=r_send.at[o, j, k],
                    recv_sem=r_recv.at[o, j, k],
                    device_id={"tensor": line(1 - o, k)},
                    device_id_type=MESH,
                ).wait_recv()

    def collect(o, kind, lo):
        total = part_in[o, 0, kind, :, lo:].astype(F32)
        for k in range(1, side):
            total = total + part_in[o, k, kind, :, lo:].astype(F32)
        return total

    skip = 2 * half - width
    tan_left = collect(0, 1, 0)
    tan_right = collect(1, 1, skip)
    tan_sum[:, 0:half] = tan_left
    tan_sum[:, half:width] = tan_right

    def sum_all(value):
        return jnp.sum(jnp.sum(value, axis=0, keepdims=True), axis=1, keepdims=True)

    own_squares = sum_all(tan_left * tan_left) + sum_all(tan_right * tan_right)
    squares[me] = jnp.broadcast_to(own_squares, (8, 128))

    def q_copy(t):
        return pltpu.make_async_remote_copy(
            src_ref=squares.at[me],
            dst_ref=squares.at[me],
            send_sem=q_send.at[t],
            recv_sem=q_recv.at[me],
            device_id={"tensor": t},
            device_id_type=MESH,
        )

    def q_start(i, carry):
        q_copy((me + i) % n_t).start()
        return carry

    lax.fori_loop(1, n_t, q_start, 0)
    image_out[:, 0:half] = collect(0, 0, 0).astype(LOW)
    image_out[:, half:width] = collect(1, 0, skip).astype(LOW)

    def q_wait(i, carry):
        t = (me + i) % n_t
        pltpu.make_async_remote_copy(
            src_ref=squares.at[t],
            dst_ref=squares.at[t],
            send_sem=q_send.at[t],
            recv_sem=q_recv.at[t],
            device_id={"tensor": t},
            device_id_type=MESH,
        ).wait_recv()
        return carry

    lax.fori_loop(1, n_t, q_wait, 0)
    square_sum = jnp.sum(squares[...], axis=0)[0:1, 0:1]
    divisor = jnp.sqrt(square_sum / (img * width)) + 0.1
    normal = (tan_sum[...] / divisor).astype(LOW)
    tangent_out[...] = normal
    upstream[...] = (cot[...].astype(F32) - normal.astype(F32)).astype(LOW)

    def u_copy(o, k):
        return pltpu.make_async_remote_copy(
            src_ref=upstream.at[:, pl.ds(o * offset, half)],
            dst_ref=up_all.at[o, pl.ds(place(1 - o) * rows, rows)],
            send_sem=u_send.at[o, k],
            recv_sem=u_recv.at[o, place(1 - o)],
            device_id={"tensor": line(1 - o, k)},
            device_id_type=MESH,
        )

    for o in range(2):
        own = place(1 - o)
        for i in range(1, side):
            u_copy(o, (own + i) % side).start()
        up_all[o, pl.ds(own * rows, rows), :] = upstream[:, o * offset : o * offset + half]

    for o in range(2):
        for i in range(1, side):
            k = (place(1 - o) + i) % side
            pltpu.make_async_remote_copy(
                src_ref=upstream.at[:, pl.ds(o * offset, half)],
                dst_ref=up_all.at[o, pl.ds(k * rows, rows)],
                send_sem=u_send.at[o, k],
                recv_sem=u_recv.at[o, k],
                device_id={"tensor": line(1 - o, k)},
                device_id_type=MESH,
            ).wait_recv()

    def t_copy(k):
        return pltpu.make_async_remote_copy(
            src_ref=twin_out.at[k],
            dst_ref=twin_in.at[k],
            send_sem=t_send.at[k],
            recv_sem=t_recv.at[k],
            device_id=twin(),
            device_id_type=MESH,
        )

    def g_copy(k):
        return pltpu.make_async_remote_copy(
            src_ref=grad_send.at[k],
            dst_ref=grad_in.at[place(c)],
            send_sem=g_send.at[k],
            recv_sem=g_recv.at[place(c)],
            device_id={"tensor": line(c, k)},
            device_id_type=MESH,
        )

    def for_twin(i, carry):
        k = (place(c) + i) % side
        twin_out[k] = jnp.dot(
            prim_t[1 - c, k], up_all[1 - c], preferred_element_type=F32
        ).astype(LOW)
        t_copy(k).start()
        return carry

    lax.fori_loop(1, side + 1, for_twin, 0)

    def for_line(i, carry):
        k = (place(c) + i) % side
        mine = jnp.dot(prim_t[c, k], up_all[c], preferred_element_type=F32)
        t_copy(k).wait_recv()
        grad_send[k] = (mine + twin_in[k].astype(F32)).astype(LOW)

        @pl.when(i < side)
        def _():
            g_copy(k).start()

        return carry

    lax.fori_loop(1, side + 1, for_line, 0)
    own = place(c)
    for i in range(1, side):
        k = (own + i) % side
        pltpu.make_async_remote_copy(
            src_ref=grad_send.at[k],
            dst_ref=grad_in.at[k],
            send_sem=g_send.at[k],
            recv_sem=g_recv.at[k],
            device_id={"tensor": line(c, k)},
            device_id_type=MESH,
        ).wait_recv()
    grad_in[own] = grad_send[own]
    total = grad_in[0].astype(F32)
    for k in range(1, side):
        total = total + grad_in[k].astype(F32)
    z_out[...] = total.astype(LOW)

    chunk_rows = 48
    chunk_cols = half // 2

    def chunk(k):
        return (
            pl.ds(pl.multiple_of((k // 2) * chunk_rows, 16), chunk_rows),
            pl.ds(pl.multiple_of((k % 2) * chunk_cols, 128), chunk_cols),
        )

    def z_copy(k, source):
        return pltpu.make_async_remote_copy(
            src_ref=z_out.at[chunk(k)],
            dst_ref=z_in.at[source],
            send_sem=z_send.at[k],
            recv_sem=z_recv.at[source],
            device_id={"dp": k * 2 + c},
            device_id_type=MESH,
        )

    def c_copy(k, owner):
        return pltpu.make_async_remote_copy(
            src_ref=final.at[(c,) + chunk(owner)],
            dst_ref=final.at[(c,) + chunk(owner)],
            send_sem=c_send.at[k],
            recv_sem=c_recv.at[owner],
            device_id={"dp": k * 2 + c},
            device_id_type=MESH,
        )

    def z_loop(step):
        def one(i, carry):
            step((z + i) % n_z)
            return carry

        lax.fori_loop(1, n_z, one, 0)

    z_loop(lambda k: z_copy(k, z).start())
    z_in[z] = z_out[chunk(z)]
    z_loop(lambda k: z_copy(k, k).wait_recv())
    total = z_in[0].astype(F32)
    for k in range(1, n_z):
        total = total + z_in[k].astype(F32)
    final[(c,) + chunk(z)] = (total * (1.0 / (2 * n_z))).astype(LOW)
    z_loop(lambda k: c_copy(k, z).start())
    z_loop(lambda k: c_copy(k, k).wait_recv())

    def s_copy(which):
        return pltpu.make_async_remote_copy(
            src_ref=final.at[which],
            dst_ref=final.at[which],
            send_sem=s_send,
            recv_sem=s_recv,
            device_id=twin(),
            device_id_type=MESH,
        )

    s_copy(c).start()

    def sent_in(s, carry):
        def one(i, inner):
            in_copy(s, (me + i) % n_t).wait_send()
            return inner

        lax.fori_loop(1, n_t, one, 0)
        return carry

    lax.fori_loop(0, slots, sent_in, 0)
    for i in range(1, side):
        w_copy((place(c) + i) % side).wait_send()
        g_copy((place(c) + i) % side).wait_send()
        for o in range(2):
            for s in range(slots):
                p_copy(s, o, (place(o) + i) % side).wait_send()
            for j in range(2):
                r_copy(o, j, (place(1 - o) + i) % side).wait_send()
            u_copy(o, (place(1 - o) + i) % side).wait_send()
    for k in range(side):
        f_copy(k).wait_send()
        t_copy(k).wait_send()

    def q_sent(i, carry):
        q_copy((me + i) % n_t).wait_send()
        return carry

    lax.fori_loop(1, n_t, q_sent, 0)
    z_loop(lambda k: z_copy(k, z).wait_send())
    z_loop(lambda k: c_copy(k, z).wait_send())
    s_copy(c).wait_send()
    s_copy(1 - c).wait_recv()
    grad_out[:, 0:half] = final[0].astype(F32)
    grad_out[:, half:width] = final[1, :, skip:].astype(F32)


def on_device(n_t, n_dp, qkv_img, tan_img, txt_kv, head_table, out_weight, cotangent):
    rows, width = qkv_img.shape[1], qkv_img.shape[3]
    slots = head_table.shape[1]
    side = 4
    n_z = n_dp // 2
    txt_len = txt_kv.shape[2]
    img = n_t * rows
    keys = img + txt_len
    keys_pad = -(-keys // 128) * 128
    half = -(-width // 256) * 128
    offset = width - half
    dims = (n_t, side, n_z, slots, rows, keys, keys_pad, half, offset, width, txt_len)
    dma = pltpu.SemaphoreType.DMA
    vmem = pl.BlockSpec(memory_space=pltpu.VMEM)
    lines = (2, side)
    outbox, live = pl.pallas_call(
        functools.partial(pack, n_t, slots),
        out_shape=(
            jax.ShapeDtypeStruct((slots, n_t, rows, 384), LOW),
            jax.ShapeDtypeStruct((slots, n_t, 8, 128), F32),
        ),
        in_specs=[pl.BlockSpec(memory_space=pltpu.SMEM), vmem, vmem],
        out_specs=(vmem, vmem),
    )(
        head_table.reshape(-1),
        jnp.transpose(qkv_img[0], (1, 0, 2)),
        jnp.transpose(tan_img[0], (1, 0, 2)),
    )
    return pl.pallas_call(
        functools.partial(body, dims),
        out_shape=(
            jax.ShapeDtypeStruct((rows, width), LOW),
            jax.ShapeDtypeStruct((rows, width), LOW),
            jax.ShapeDtypeStruct((slots * 64, width), F32),
        ),
        in_specs=[pl.BlockSpec(memory_space=pl.ANY)] + [vmem] * 4,
        out_specs=(vmem, vmem, vmem),
        scratch_shapes=[
            pltpu.VMEM((slots, n_t, rows, 384), LOW),
            pltpu.VMEM((384, 256), LOW),
            pltpu.VMEM((slots, 128, 2 * keys_pad), LOW),
            pltpu.VMEM((slots, 2 * keys_pad, 128), LOW),
            pltpu.VMEM((slots, side, side, rows, 128), LOW),
            pltpu.VMEM((2, slots, side, side, rows, 128), LOW),
            pltpu.VMEM((2, side * 256, half), LOW),
            pltpu.VMEM((2, 2 * side * rows, side * 256), LOW),
            pltpu.VMEM((2, side, 192, side * rows), LOW),
            pltpu.VMEM((2, side, 2, rows, half), LOW),
            pltpu.VMEM((2, side, 2, rows, half), LOW),
            pltpu.VMEM((rows, width), F32),
            pltpu.VMEM((n_t, 8, 128), F32),
            pltpu.VMEM((rows, width), LOW),
            pltpu.VMEM((2, side * rows, half), LOW),
            pltpu.VMEM((side, 192, half), LOW),
            pltpu.VMEM((side, 192, half), LOW),
            pltpu.VMEM((side, 192, half), LOW),
            pltpu.VMEM((side, 192, half), LOW),
            pltpu.VMEM((192, half), LOW),
            pltpu.VMEM((n_z, 48, half // 2), LOW),
            pltpu.VMEM((2, 192, half), LOW),
            dma((slots, n_t)),
            dma((slots, n_t)),
            dma((side,)),
            dma((side,)),
            dma((side,)),
            dma((side,)),
            dma((1 + slots,)),
            dma((2, slots, side)),
            dma((2, slots, side)),
            dma((2, 2, side)),
            dma((2, 2, side)),
            dma((n_t,)),
            dma((n_t,)),
            dma(lines),
            dma(lines),
            dma((side,)),
            dma((side,)),
            dma((side,)),
            dma((side,)),
            dma((n_z,)),
            dma((n_z,)),
            dma((n_z,)),
            dma((n_z,)),
            dma,
            dma,
        ],
        compiler_params=pltpu.CompilerParams(
            collective_id=0, has_side_effects=True, vmem_limit_bytes=56 * 1024 * 1024
        ),
    )(
        outbox,
        live,
        txt_kv[0],
        out_weight,
        cotangent[0],
    )


def solution(mesh):
    n_t, n_dp = mesh.shape["tensor"], mesh.shape["dp"]

    def step(*args):
        image_out, tangent_out, weight_grad = on_device(n_t, n_dp, *args)
        return image_out[None], tangent_out[None], weight_grad

    return jax.shard_map(
        step,
        mesh=mesh,
        in_specs=(
            P("dp", "tensor", None, None),
            P("dp", "tensor", None, None),
            P("dp", "tensor", None, None),
            P(),
            P("tensor", None),
            P("dp", "tensor", None),
        ),
        out_specs=(P("dp", "tensor", None), P("dp", "tensor", None), P("tensor", None)),
        check_vma=False,
    )
```

```python
import functools

import jax
import jax.numpy as jnp
from jax import lax
from jax.experimental import pallas as pl
from jax.experimental.pallas import tpu as pltpu
from jax.sharding import PartitionSpec as P

MESH = pl.DeviceIdType.MESH
F32 = jnp.float32
LOW = jnp.bfloat16


def swap_halves(value):
    return pltpu.roll(value, 64, 1)


def finish(image, tangent, grad, image_out, tangent_out, grad_out):
    half = 2 * grad.shape[3]
    part = grad.shape[3]
    width = image.shape[1]
    image_out[...] = image[...]
    tangent_out[...] = tangent[...]
    grad_out[:, 0:part] = grad[0, 0].astype(F32)
    grad_out[:, part:half] = grad[0, 1].astype(F32)
    skip = 2 * half - width
    grad_out[:, half : half + part - skip] = grad[1, 0, :, skip:].astype(F32)
    grad_out[:, half + part - skip : width] = grad[1, 1].astype(F32)


def body(
    dims,
    table,
    qkv,
    tan,
    txt,
    weight,
    cot,
    image_out,
    tangent_out,
    grad_out,
    cot_local,
    staged,
    outbox,
    arrived,
    text_pad,
    score_rhs,
    value_rhs,
    attn,
    regroup,
    group_weight,
    proj_lhs,
    prim_t,
    part_out,
    part_in,
    tan_sum,
    squares,
    upstream,
    up_all,
    twin_out,
    twin_in,
    grad_send,
    grad_in,
    z_out,
    z_in,
    final,
    a_send,
    a_recv,
    w_send,
    w_recv,
    x_send,
    x_recv,
    f_send,
    f_recv,
    own_sem,
    p_send,
    p_recv,
    r_send,
    r_recv,
    q_send,
    q_recv,
    u_send,
    u_recv,
    t_send,
    t_recv,
    g_send,
    g_recv,
    z_send,
    z_recv,
    c_send,
    c_recv,
    s_send,
    s_recv,
):
    n_t, side, n_z, slots, rows, keys, keys_pad, half, offset, width, txt_len = dims
    me = lax.axis_index("tensor")
    dp = lax.axis_index("dp")
    x = me // side
    y = me % side
    z = dp // 2
    c = dp % 2
    img = n_t * rows
    group_rows = side * rows

    def line(o, k):
        return (1 - o) * (x * side + k) + o * (k * side + y)

    def place(o):
        return (1 - o) * y + o * x

    def twin():
        return {"dp": z * 2 + (1 - c)}

    low_half = lax.broadcasted_iota(jnp.int32, (1, 128), 1) < 64

    barrier = pltpu.get_barrier_semaphore()

    def greet(i, carry):
        t = ((x + i // side) % side) * side + (y + i % side) % side
        pl.semaphore_signal(barrier, inc=1, device_id={"tensor": t}, device_id_type=MESH)
        return carry

    lax.fori_loop(1, n_t, greet, 0)

    def greet_z(i, carry):
        pl.semaphore_signal(
            barrier, inc=1, device_id={"dp": ((z + i) % n_z) * 2 + c}, device_id_type=MESH
        )
        return carry

    lax.fori_loop(1, n_z, greet_z, 0)
    pl.semaphore_signal(barrier, inc=1, device_id=twin(), device_id_type=MESH)
    cot_copy = pltpu.make_async_copy(cot, cot_local, own_sem.at[1 + slots])
    cot_copy.start()

    for o in range(2):
        for k in range(side):
            group_weight[o, k * 256 + 192 : k * 256 + 256, :] = jnp.zeros((64, half), LOW)

    def text_rows(s):
        text_pad[320:384, :] = jnp.zeros((64, 256), LOW)
        text_pad[0:txt_len, :] = txt[s]
        kv = text_pad[:, 0:128].astype(F32)
        dkv = text_pad[:, 128:256].astype(F32)
        key_pair = jnp.where(low_half, kv, swap_halves(dkv))
        val_pair = jnp.where(low_half, swap_halves(kv), dkv)
        key_t = key_pair.T.astype(LOW)
        score_rhs[s, 0:64, 0:keys_pad] = jnp.zeros((64, keys_pad), LOW)
        score_rhs[s, 64:128, img:keys_pad] = key_t[0:64]
        score_rhs[s, :, keys_pad + img : 2 * keys_pad] = key_t
        value_rhs[s, img:keys_pad, :] = val_pair.astype(LOW)
        value_rhs[s, keys_pad + img : 2 * keys_pad, :] = jnp.where(low_half, 0.0, kv).astype(LOW)

    for kind in range(3):
        for page in range(width // 128):
            staged[kind, page] = qkv[kind, :, page * 128 : page * 128 + 128]
            staged[3 + kind, page] = tan[kind, :, page * 128 : page * 128 + 128]

    def pick(s, t):
        head = jnp.maximum(table[s, t], 0)
        page = lax.shift_right_logical(head, 1)
        odd = jnp.full((1, 128), lax.bitwise_and(head, 1), jnp.int32) == 1

        def pair(first, second):
            a = staged[first, page]
            b = staged[second, page]
            return jnp.where(
                low_half, jnp.where(odd, swap_halves(a), a), jnp.where(odd, b, swap_halves(b))
            )

        outbox[s, t, :, 0:128] = pair(3, 0) * jnp.asarray(0.125, LOW)
        outbox[s, t, :, 128:256] = pair(1, 4)
        outbox[s, t, :, 256:384] = pair(2, 5)

    pl.semaphore_wait(barrier, n_t + n_z - 1)

    def in_copy(s, t):
        return pltpu.make_async_remote_copy(
            src_ref=outbox.at[s, t],
            dst_ref=arrived.at[s, me],
            send_sem=a_send.at[s, t],
            recv_sem=a_recv.at[s, me],
            device_id={"tensor": t},
            device_id_type=MESH,
        )

    def ring(step):
        def one(i, carry):
            step(((x + i // side) % side) * side + (y + i % side) % side)
            return carry

        lax.fori_loop(1, n_t, one, 0)

    def in_own(s):
        return pltpu.make_async_copy(outbox.at[s, me], arrived.at[s, me], own_sem.at[1 + s])

    half_at = pl.multiple_of(c * offset, 128)

    chunk_rows = 2 * 192 // n_z
    chunk_cols = half // 2

    def w_span(k, at):
        return (
            pl.ds(pl.multiple_of(k * 256 + (at // 2) * chunk_rows, 16), chunk_rows),
            pl.ds(pl.multiple_of((at % 2) * chunk_cols, 128), chunk_cols),
        )

    def w_copy(k):
        return pltpu.make_async_remote_copy(
            src_ref=weight.at[
                pl.ds(pl.multiple_of((z // 2) * chunk_rows, 16), chunk_rows),
                pl.ds(pl.multiple_of(c * offset + (z % 2) * chunk_cols, 128), chunk_cols),
            ],
            dst_ref=group_weight.at[(c,) + w_span(place(c), z)],
            send_sem=w_send.at[k],
            recv_sem=w_recv.at[place(c)],
            device_id={"tensor": line(c, k)},
            device_id_type=MESH,
        )

    def w_arrival(k):
        return pltpu.make_async_remote_copy(
            src_ref=group_weight.at[(c,) + w_span(k, z)],
            dst_ref=group_weight.at[(c,) + w_span(k, z)],
            send_sem=w_send.at[k],
            recv_sem=w_recv.at[k],
            device_id={"tensor": line(c, k)},
            device_id_type=MESH,
        )

    def x_copy(k, at, other):
        return pltpu.make_async_remote_copy(
            src_ref=group_weight.at[(c,) + w_span(k, at)],
            dst_ref=group_weight.at[(c,) + w_span(k, at)],
            send_sem=x_send.at[k, other],
            recv_sem=x_recv.at[k, at],
            device_id={"dp": other * 2 + c},
            device_id_type=MESH,
        )

    def x_loop(step):
        def one(i, carry):
            for n in range(1, side):
                step((place(c) + n) % side, (z + i) % n_z)
            return carry

        lax.fori_loop(1, n_z, one, 0)

    def w_own():
        return pltpu.make_async_copy(
            weight.at[:, pl.ds(half_at, half)],
            group_weight.at[c, pl.ds(place(c) * 256, 192)],
            own_sem.at[0],
        )

    def f_copy(k):
        return pltpu.make_async_remote_copy(
            src_ref=group_weight.at[c, pl.ds(k * 256, 192)],
            dst_ref=group_weight.at[c, pl.ds(k * 256, 192)],
            send_sem=f_send.at[k],
            recv_sem=f_recv.at[k],
            device_id=twin(),
            device_id_type=MESH,
        )

    def f_arrival(k):
        return pltpu.make_async_remote_copy(
            src_ref=group_weight.at[1 - c, pl.ds(k * 256, 192)],
            dst_ref=group_weight.at[1 - c, pl.ds(k * 256, 192)],
            send_sem=f_send.at[k],
            recv_sem=f_recv.at[k],
            device_id=twin(),
            device_id_type=MESH,
        )

    w_own().start()
    for i in range(1, side):
        w_copy((place(c) + i) % side).start()

    def depart(s):
        def one(t):
            pick(s, t)
            in_copy(s, t).start()

        ring(one)

    depart(0)
    depart(1)
    ring(lambda t: pick(2, t))
    for s in range(slots):
        pick(s, me)
        in_own(s).start()
        text_rows(s)

    for i in range(1, side):
        w_arrival((place(c) + i) % side).wait_recv()
    x_loop(lambda k, other: x_copy(k, z, other).start())

    def p_copy(s, o, k):
        source = attn.at[s, :, k] if o == 0 else attn.at[s, k]
        return pltpu.make_async_remote_copy(
            src_ref=source,
            dst_ref=regroup.at[o, s, place(o)],
            send_sem=p_send.at[o, s, k],
            recv_sem=p_recv.at[o, s, place(o)],
            device_id={"tensor": line(o, k)},
            device_id_type=MESH,
        )

    def one_slot(s, carry):
        @pl.when(s == 0)
        def _():
            def step(t):
                in_copy(0, t).wait_send()
                in_copy(2, t).start()

            ring(step)

        def arrival(i, inner):
            t = (me + i) % n_t
            pltpu.make_async_remote_copy(
                src_ref=outbox.at[s, t],
                dst_ref=arrived.at[s, t],
                send_sem=a_send.at[s, t],
                recv_sem=a_recv.at[s, t],
                device_id={"tensor": t},
                device_id_type=MESH,
            ).wait_recv()
            return inner

        lax.fori_loop(1, n_t, arrival, 0)
        in_own(s).wait()
        key_t = arrived[s, :, :, 128:256].reshape(img, 128).astype(F32).T.astype(LOW)
        score_rhs[s, 64:128, 0:img] = key_t[0:64]
        score_rhs[s, :, keys_pad : keys_pad + img] = key_t
        val_pair = arrived[s, :, :, 256:384].reshape(img, 128)
        value_rhs[s, 0:img, :] = val_pair
        value_rhs[s, keys_pad : keys_pad + img, :] = jnp.where(
            low_half, 0.0, swap_halves(val_pair.astype(F32))
        ).astype(LOW)
        filled = jnp.where(jnp.full((1, 128), table[s, me], jnp.int32) >= 0, 1.0, 0.0)

        def one_block(q, inner):
            lhs = arrived[s, pl.ds(q * side, side), :, 0:128].reshape(group_rows, 128)
            scores = jnp.dot(lhs, score_rhs[s, :, 0:keys_pad], preferred_element_type=F32)
            tangents = jnp.dot(
                lhs, score_rhs[s, :, keys_pad : 2 * keys_pad], preferred_element_type=F32
            )
            valid = lax.broadcasted_iota(jnp.int32, (1, 128), 1) < keys - (keys_pad - 128)
            scores = jnp.concatenate(
                [
                    scores[:, : keys_pad - 128],
                    jnp.where(valid, scores[:, keys_pad - 128 :], -1e30),
                ],
                1,
            )
            top = jnp.max(scores, axis=1, keepdims=True)
            raised = jnp.exp(scores - top)
            total = jnp.sum(raised, axis=1, keepdims=True)
            mean = jnp.sum(raised * tangents, axis=1, keepdims=True) / total
            shifted = raised * (tangents - mean)
            joined = jnp.dot(
                raised.astype(LOW), value_rhs[s, 0:keys_pad, :], preferred_element_type=F32
            ) + jnp.dot(
                shifted.astype(LOW),
                value_rhs[s, keys_pad : 2 * keys_pad, :],
                preferred_element_type=F32,
            )
            joined = (joined / total * filled).astype(LOW)
            attn[s, q] = joined.reshape(side, rows, 128)
            return inner

        lax.fori_loop(0, side, one_block, 0)
        for o in range(2):
            own = place(o)
            for i in range(1, side):
                p_copy(s, o, (own + i) % side).start()
        regroup[0, s, y] = attn[s, :, y]
        regroup[1, s, x] = attn[s, x]

        return carry

    lax.fori_loop(0, slots, one_slot, 0)

    w_own().wait()
    x_loop(lambda k, other: x_copy(k, other, other).wait_recv())
    for k in range(side):
        f_copy(k).start()

    def r_copy(kind, o, j, k):
        span = pl.ds(pl.multiple_of(j * 256, 256), 256)
        return pltpu.make_async_remote_copy(
            src_ref=part_out.at[kind, o, k, :, span],
            dst_ref=part_in.at[kind, o, place(1 - o), :, span],
            send_sem=r_send.at[kind, o, j, k],
            recv_sem=r_recv.at[kind, o, j, place(1 - o)],
            device_id={"tensor": line(1 - o, k)},
            device_id_type=MESH,
        )

    def r_arrival(kind, o, j, k):
        span = pl.ds(pl.multiple_of(j * 256, 256), 256)
        return pltpu.make_async_remote_copy(
            src_ref=part_out.at[kind, o, k, :, span],
            dst_ref=part_in.at[kind, o, k, :, span],
            send_sem=r_send.at[kind, o, j, k],
            recv_sem=r_recv.at[kind, o, j, k],
            device_id={"tensor": line(1 - o, k)},
            device_id_type=MESH,
        )

    for o in range(2):
        for s in range(slots):
            for i in range(1, side):
                k = (place(o) + i) % side
                pltpu.make_async_remote_copy(
                    src_ref=regroup.at[o, s, k],
                    dst_ref=regroup.at[o, s, k],
                    send_sem=p_send.at[o, s, k],
                    recv_sem=p_recv.at[o, s, k],
                    device_id={"tensor": line(o, k)},
                    device_id_type=MESH,
                ).wait_recv()

        def tangents_of(k, carry, o=o):
            first = regroup[o, 0, k].reshape(group_rows, 128).astype(F32)
            second = regroup[o, 1, k].reshape(group_rows, 128).astype(F32)
            third = regroup[o, 2, k].reshape(group_rows, 128).astype(F32)
            tang = jnp.where(low_half, swap_halves(first), second)
            tang_last = jnp.where(low_half, swap_halves(third), 0.0)
            at = pl.multiple_of(k * 256, 256)
            proj_lhs[1, o, :, pl.ds(at, 128)] = tang.astype(LOW)
            proj_lhs[1, o, :, pl.ds(at + 128, 128)] = tang_last.astype(LOW)
            return carry

        lax.fori_loop(0, side, tangents_of, 0)

    for k in range(side):
        f_arrival(k).wait_recv()

    steps = half // 256

    def project(kind):
        def one(n, carry):
            o = n % 2
            j = n // 2
            span = pl.ds(pl.multiple_of(j * 256, 256), 256)
            part = jnp.dot(
                proj_lhs[kind, o], group_weight[o, :, span], preferred_element_type=F32
            ).astype(LOW)
            for k in range(side):
                part_out[kind, o, k, :, span] = part[k * rows : (k + 1) * rows]
            own = place(1 - o)
            for i in range(1, side):
                r_copy(kind, o, j, (own + i) % side).start()
            part_in[kind, o, own, :, span] = part_out[kind, o, own, :, span]
            return carry

        lax.fori_loop(0, 2 * steps, one, 0)

    def gathered(kind):
        def one(n, carry):
            for i in range(1, side):
                r_arrival(kind, n % 2, n // 2, (place(1 - n % 2) + i) % side).wait_recv()
            return carry

        lax.fori_loop(0, 2 * steps, one, 0)

    project(1)

    for o in range(2):

        def prims_of(k, carry, o=o):
            first = regroup[o, 0, k].reshape(group_rows, 128).astype(F32)
            second = regroup[o, 1, k].reshape(group_rows, 128).astype(F32)
            third = regroup[o, 2, k].reshape(group_rows, 128).astype(F32)
            prim = jnp.where(low_half, first, swap_halves(second))
            prim_last = jnp.where(low_half, third, 0.0)
            at = pl.multiple_of(k * 256, 256)
            proj_lhs[0, o, :, pl.ds(at, 128)] = prim.astype(LOW)
            proj_lhs[0, o, :, pl.ds(at + 128, 128)] = prim_last.astype(LOW)
            prim_t[o, k, 0:128, :] = prim.T.astype(LOW)
            prim_t[o, k, 128:192, :] = prim_last.T[0:64].astype(LOW)
            return carry

        lax.fori_loop(0, side, prims_of, 0)

    gathered(1)

    def collect(o, kind, lo):
        total = part_in[kind, o, 0, :, lo:].astype(F32)
        for k in range(1, side):
            total = total + part_in[kind, o, k, :, lo:].astype(F32)
        return total

    skip = 2 * half - width
    tan_left = collect(0, 1, 0)
    tan_right = collect(1, 1, skip)
    tan_sum[:, 0:half] = tan_left
    tan_sum[:, half:width] = tan_right

    def sum_all(value):
        return jnp.sum(jnp.sum(value, axis=0, keepdims=True), axis=1, keepdims=True)

    own_squares = sum_all(tan_left * tan_left) + sum_all(tan_right * tan_right)
    squares[me] = jnp.broadcast_to(own_squares, (8, 128))

    def q_copy(t):
        return pltpu.make_async_remote_copy(
            src_ref=squares.at[me],
            dst_ref=squares.at[me],
            send_sem=q_send.at[t],
            recv_sem=q_recv.at[me],
            device_id={"tensor": t},
            device_id_type=MESH,
        )

    def q_start(i, carry):
        q_copy((me + i) % n_t).start()
        return carry

    lax.fori_loop(1, n_t, q_start, 0)
    def q_wait(i, carry):
        t = (me + i) % n_t
        pltpu.make_async_remote_copy(
            src_ref=squares.at[t],
            dst_ref=squares.at[t],
            send_sem=q_send.at[t],
            recv_sem=q_recv.at[t],
            device_id={"tensor": t},
            device_id_type=MESH,
        ).wait_recv()
        return carry

    lax.fori_loop(1, n_t, q_wait, 0)
    square_sum = jnp.sum(squares[...], axis=0)[0:1, 0:1]
    divisor = jnp.sqrt(square_sum / (img * width)) + 0.1
    normal = (tan_sum[...] / divisor).astype(LOW)
    tangent_out[...] = normal
    cot_copy.wait()
    upstream[...] = (cot_local[...].astype(F32) - normal.astype(F32)).astype(LOW)

    part = half // 2

    def u_copy(o, j, k):
        return pltpu.make_async_remote_copy(
            src_ref=upstream.at[:, pl.ds(o * offset + j * part, part)],
            dst_ref=up_all.at[o, j, pl.ds(place(1 - o) * rows, rows)],
            send_sem=u_send.at[o, j, k],
            recv_sem=u_recv.at[o, j, place(1 - o)],
            device_id={"tensor": line(1 - o, k)},
            device_id_type=MESH,
        )

    for j in range(2):
        for i in range(1, side):
            for o in range(2):
                u_copy(o, j, (place(1 - o) + i) % side).start()
    for j in range(2):
        for o in range(2):
            at = o * offset + j * part
            up_all[o, j, pl.ds(place(1 - o) * rows, rows), :] = upstream[:, at : at + part]

    def t_copy(j, k):
        return pltpu.make_async_remote_copy(
            src_ref=twin_out.at[j, k],
            dst_ref=twin_in.at[j, k],
            send_sem=t_send.at[j, k],
            recv_sem=t_recv.at[j, k],
            device_id=twin(),
            device_id_type=MESH,
        )

    def g_copy(j, k):
        return pltpu.make_async_remote_copy(
            src_ref=grad_send.at[j, k],
            dst_ref=grad_in.at[j, place(c)],
            send_sem=g_send.at[j, k],
            recv_sem=g_recv.at[j, place(c)],
            device_id={"tensor": line(c, k)},
            device_id_type=MESH,
        )

    own = place(c)

    def grad_part(j, carry):
        for o in range(2):
            for i in range(1, side):
                k = (place(1 - o) + i) % side
                pltpu.make_async_remote_copy(
                    src_ref=upstream.at[:, pl.ds(o * offset, part)],
                    dst_ref=up_all.at[o, j, pl.ds(k * rows, rows)],
                    send_sem=u_send.at[o, j, k],
                    recv_sem=u_recv.at[o, j, k],
                    device_id={"tensor": line(1 - o, k)},
                    device_id_type=MESH,
                ).wait_recv()

        def for_twin(i, inner):
            k = (own + i) % side
            twin_out[j, k] = jnp.dot(
                prim_t[1 - c, k], up_all[1 - c, j], preferred_element_type=F32
            ).astype(LOW)
            t_copy(j, k).start()
            return inner

        lax.fori_loop(1, side + 1, for_twin, 0)

        def for_line(i, inner):
            k = (own + i) % side
            mine = jnp.dot(prim_t[c, k], up_all[c, j], preferred_element_type=F32)
            t_copy(j, k).wait_recv()
            grad_send[j, k] = (mine + twin_in[j, k].astype(F32)).astype(LOW)

            @pl.when(i < side)
            def _():
                g_copy(j, k).start()

            return inner

        lax.fori_loop(1, side + 1, for_line, 0)
        grad_in[j, own] = grad_send[j, own]
        return carry

    lax.fori_loop(0, 2, grad_part, 0)

    def chunk(k):
        return (k % 2, pl.ds(pl.multiple_of((k // 2) * chunk_rows, 16), chunk_rows))

    def z_copy(k, source):
        return pltpu.make_async_remote_copy(
            src_ref=z_out.at[chunk(k)],
            dst_ref=z_in.at[source],
            send_sem=z_send.at[k],
            recv_sem=z_recv.at[source],
            device_id={"dp": k * 2 + c},
            device_id_type=MESH,
        )

    def c_copy(k, owner):
        return pltpu.make_async_remote_copy(
            src_ref=final.at[(c,) + chunk(owner)],
            dst_ref=final.at[(c,) + chunk(owner)],
            send_sem=c_send.at[k],
            recv_sem=c_recv.at[owner],
            device_id={"dp": k * 2 + c},
            device_id_type=MESH,
        )

    def z_loop(step):
        def one(i, carry):
            step((z + i) % n_z)
            return carry

        lax.fori_loop(1, n_z, one, 0)

    def to_owners(j, carry):
        for i in range(1, side):
            k = (own + i) % side
            pltpu.make_async_remote_copy(
                src_ref=grad_send.at[j, k],
                dst_ref=grad_in.at[j, k],
                send_sem=g_send.at[j, k],
                recv_sem=g_recv.at[j, k],
                device_id={"tensor": line(c, k)},
                device_id_type=MESH,
            ).wait_recv()
        total = grad_in[j, 0].astype(F32)
        for k in range(1, side):
            total = total + grad_in[j, k].astype(F32)
        z_out[j] = total.astype(LOW)

        def one(i, inner):
            k = (z + i) % n_z

            @pl.when(k % 2 == j)
            def _():
                z_copy(k, z).start()

            return inner

        lax.fori_loop(1, n_z, one, 0)
        return carry

    lax.fori_loop(0, 2, to_owners, 0)

    project(0)

    z_in[z] = z_out[chunk(z)]
    z_loop(lambda k: z_copy(k, k).wait_recv())
    total = z_in[0].astype(F32)
    for k in range(1, n_z):
        total = total + z_in[k].astype(F32)
    final[(c,) + chunk(z)] = (total * (1.0 / (2 * n_z))).astype(LOW)
    z_loop(lambda k: c_copy(k, z).start())
    gathered(0)
    image_out[:, 0:half] = collect(0, 0, 0).astype(LOW)
    image_out[:, half:width] = collect(1, 0, skip).astype(LOW)
    z_loop(lambda k: c_copy(k, k).wait_recv())

    def s_copy(which):
        return pltpu.make_async_remote_copy(
            src_ref=final.at[which],
            dst_ref=final.at[which],
            send_sem=s_send,
            recv_sem=s_recv,
            device_id=twin(),
            device_id_type=MESH,
        )

    s_copy(c).start()

    ring(lambda t: in_copy(1, t).wait_send())
    ring(lambda t: in_copy(2, t).wait_send())
    x_loop(lambda k, other: x_copy(k, z, other).wait_send())
    for i in range(1, side):
        w_copy((place(c) + i) % side).wait_send()
        for o in range(2):
            for s in range(slots):
                p_copy(s, o, (place(o) + i) % side).wait_send()
            for j in range(2):
                u_copy(o, j, (place(1 - o) + i) % side).wait_send()
        for j in range(2):
            g_copy(j, (place(c) + i) % side).wait_send()

    def r_sent(n, carry):
        o = n % 2
        for kind in range(2):
            for i in range(1, side):
                r_copy(kind, o, n // 2, (place(1 - o) + i) % side).wait_send()
        return carry

    lax.fori_loop(0, 2 * steps, r_sent, 0)
    for k in range(side):
        f_copy(k).wait_send()
        for j in range(2):
            t_copy(j, k).wait_send()

    def q_sent(i, carry):
        q_copy((me + i) % n_t).wait_send()
        return carry

    lax.fori_loop(1, n_t, q_sent, 0)
    z_loop(lambda k: z_copy(k, z).wait_send())
    z_loop(lambda k: c_copy(k, z).wait_send())
    s_copy(c).wait_send()
    s_copy(1 - c).wait_recv()
    grad_out[...] = final[...]


def on_device(n_t, n_dp, qkv_img, tan_img, txt_kv, head_table, out_weight, cotangent):
    rows, width = qkv_img.shape[1], qkv_img.shape[3]
    slots = head_table.shape[1]
    side = 4
    n_z = n_dp // 2
    txt_len = txt_kv.shape[2]
    img = n_t * rows
    keys = img + txt_len
    keys_pad = -(-keys // 128) * 128
    half = -(-width // 256) * 128
    offset = width - half
    dims = (n_t, side, n_z, slots, rows, keys, keys_pad, half, offset, width, txt_len)
    dma = pltpu.SemaphoreType.DMA
    vmem = pl.BlockSpec(memory_space=pltpu.VMEM)
    hbm = pl.BlockSpec(memory_space=pl.ANY)
    steps = half // 256
    image, tangent, grad = pl.pallas_call(
        functools.partial(body, dims),
        out_shape=(
            jax.ShapeDtypeStruct((rows, width), LOW),
            jax.ShapeDtypeStruct((rows, width), LOW),
            jax.ShapeDtypeStruct((2, 2, 192, half // 2), LOW),
        ),
        in_specs=[pl.BlockSpec(memory_space=pltpu.SMEM), vmem, vmem, vmem, hbm, hbm],
        out_specs=(vmem, vmem, vmem),
        scratch_shapes=[
            pltpu.VMEM((rows, width), LOW),
            pltpu.VMEM((6, width // 128, rows, 128), LOW),
            pltpu.VMEM((slots, n_t, rows, 384), LOW),
            pltpu.VMEM((slots, n_t, rows, 384), LOW),
            pltpu.VMEM((384, 256), LOW),
            pltpu.VMEM((slots, 128, 2 * keys_pad), LOW),
            pltpu.VMEM((slots, 2 * keys_pad, 128), LOW),
            pltpu.VMEM((slots, side, side, rows, 128), LOW),
            pltpu.VMEM((2, slots, side, side, rows, 128), LOW),
            pltpu.VMEM((2, side * 256, half), LOW),
            pltpu.VMEM((2, 2, side * rows, side * 256), LOW),
            pltpu.VMEM((2, side, 192, side * rows), LOW),
            pltpu.VMEM((2, 2, side, rows, half), LOW),
            pltpu.VMEM((2, 2, side, rows, half), LOW),
            pltpu.VMEM((rows, width), F32),
            pltpu.VMEM((n_t, 8, 128), F32),
            pltpu.VMEM((rows, width), LOW),
            pltpu.VMEM((2, 2, side * rows, half // 2), LOW),
            pltpu.VMEM((2, side, 192, half // 2), LOW),
            pltpu.VMEM((2, side, 192, half // 2), LOW),
            pltpu.VMEM((2, side, 192, half // 2), LOW),
            pltpu.VMEM((2, side, 192, half // 2), LOW),
            pltpu.VMEM((2, 192, half // 2), LOW),
            pltpu.VMEM((n_z, 2 * 192 // n_z, half // 2), LOW),
            pltpu.VMEM((2, 2, 192, half // 2), LOW),
            dma((slots, n_t)),
            dma((slots, n_t)),
            dma((side,)),
            dma((side,)),
            dma((side, n_z)),
            dma((side, n_z)),
            dma((side,)),
            dma((side,)),
            dma((2 + slots,)),
            dma((2, slots, side)),
            dma((2, slots, side)),
            dma((2, 2, steps, side)),
            dma((2, 2, steps, side)),
            dma((n_t,)),
            dma((n_t,)),
            dma((2, 2, side)),
            dma((2, 2, side)),
            dma((2, side)),
            dma((2, side)),
            dma((2, side)),
            dma((2, side)),
            dma((n_z,)),
            dma((n_z,)),
            dma((n_z,)),
            dma((n_z,)),
            dma,
            dma,
        ],
        compiler_params=pltpu.CompilerParams(
            collective_id=0, has_side_effects=True, vmem_limit_bytes=56 * 1024 * 1024
        ),
    )(
        head_table.T,
        jnp.transpose(qkv_img[0], (1, 0, 2)),
        jnp.transpose(tan_img[0], (1, 0, 2)),
        txt_kv[0],
        out_weight,
        cotangent[0],
    )
    parts = 4
    by_rows = pl.BlockSpec((rows // parts, width), lambda i: (i, 0))
    return pl.pallas_call(
        finish,
        grid=(parts,),
        out_shape=(
            jax.ShapeDtypeStruct((rows, width), LOW),
            jax.ShapeDtypeStruct((rows, width), LOW),
            jax.ShapeDtypeStruct((slots * 64, width), F32),
        ),
        in_specs=[
            by_rows,
            by_rows,
            pl.BlockSpec((2, 2, 192 // parts, half // 2), lambda i: (0, 0, i, 0)),
        ],
        out_specs=(by_rows, by_rows, pl.BlockSpec((192 // parts, width), lambda i: (i, 0))),
    )(image, tangent, grad)


def solution(mesh):
    n_t, n_dp = mesh.shape["tensor"], mesh.shape["dp"]

    def step(*args):
        image_out, tangent_out, weight_grad = on_device(n_t, n_dp, *args)
        return image_out[None], tangent_out[None], weight_grad

    return jax.shard_map(
        step,
        mesh=mesh,
        in_specs=(
            P("dp", "tensor", None, None),
            P("dp", "tensor", None, None),
            P("dp", "tensor", None, None),
            P(),
            P("tensor", None),
            P("dp", "tensor", None),
        ),
        out_specs=(P("dp", "tensor", None), P("dp", "tensor", None), P("tensor", None)),
        check_vma=False,
    )
```

```python
import functools

import jax
import jax.numpy as jnp
from jax import lax
from jax.experimental import pallas as pl
from jax.experimental.pallas import tpu as pltpu
from jax.sharding import PartitionSpec as P

MESH = pl.DeviceIdType.MESH
F32 = jnp.float32
LOW = jnp.bfloat16


def swap_halves(value):
    return pltpu.roll(value, 64, 1)


def finish(
    image, tangent, grad, image_out, tangent_out, grad_out, pair, held, wide, in_sem, out_sem, way_sem
):
    half = grad.shape[2]
    width = image.shape[1]
    skip = 2 * half - width
    blocks = 4
    tall = grad.shape[1] // blocks

    def load(i):
        rows = pl.ds(i * tall, tall)
        return pltpu.make_async_copy(grad.at[:, rows], held.at[:, rows], in_sem.at[i])

    def store(i):
        rows = pl.ds(i * tall, tall)
        return pltpu.make_async_copy(wide.at[rows], grad_out.at[rows], out_sem.at[i])

    for i in range(blocks):
        load(i).start()
    there = (
        pltpu.make_async_copy(image, pair.at[0], way_sem.at[0]),
        pltpu.make_async_copy(tangent, pair.at[1], way_sem.at[1]),
    )
    back = (
        pltpu.make_async_copy(pair.at[0], image_out, way_sem.at[2]),
        pltpu.make_async_copy(pair.at[1], tangent_out, way_sem.at[3]),
    )
    for copy in there:
        copy.start()
    for i in range(blocks):
        load(i).wait()
        rows = pl.ds(i * tall, tall)
        wide[rows, 0:half] = held[0, rows].astype(F32)
        wide[rows, half:width] = held[1, rows, skip:].astype(F32)
        store(i).start()
    for copy, after in zip(there, back):
        copy.wait()
        after.start()
    for i in range(blocks):
        store(i).wait()
    for copy in back:
        copy.wait()


def body(
    dims,
    table,
    qkv,
    tan,
    txt,
    weight,
    cot,
    image_out,
    tangent_out,
    grad_out,
    cot_local,
    qkv_local,
    tan_local,
    txt_local,
    staged,
    outbox,
    arrived,
    text_pad,
    score_rhs,
    value_rhs,
    attn,
    regroup,
    group_weight,
    proj_lhs,
    prim_t,
    part_out,
    part_in,
    tan_sum,
    squares,
    upstream,
    up_all,
    twin_out,
    twin_in,
    grad_send,
    grad_in,
    z_out,
    z_in,
    final,
    a_send,
    a_recv,
    w_send,
    w_recv,
    x_send,
    x_recv,
    f_send,
    f_recv,
    own_sem,
    p_send,
    p_recv,
    r_send,
    r_recv,
    q_send,
    q_recv,
    u_send,
    u_recv,
    t_send,
    t_recv,
    g_send,
    g_recv,
    z_send,
    z_recv,
    c_send,
    c_recv,
    s_send,
    s_recv,
):
    n_t, side, n_z, slots, rows, keys, keys_pad, half, offset, width, txt_len = dims
    me = lax.axis_index("tensor")
    dp = lax.axis_index("dp")
    x = me // side
    y = me % side
    z = dp // 2
    c = dp % 2
    img = n_t * rows
    group_rows = side * rows

    def line(o, k):
        return (1 - o) * (x * side + k) + o * (k * side + y)

    def place(o):
        return (1 - o) * y + o * x

    def twin():
        return {"dp": z * 2 + (1 - c)}

    low_half = lax.broadcasted_iota(jnp.int32, (1, 128), 1) < 64

    cot_copy = pltpu.make_async_copy(cot, cot_local, own_sem.at[1 + slots])
    txt_copy = pltpu.make_async_copy(txt, txt_local, own_sem.at[2 + slots])
    loads = [
        pltpu.make_async_copy(whole.at[kind], local.at[kind], own_sem.at[3 + slots + 3 * n + kind])
        for n, (whole, local) in enumerate(((qkv, qkv_local), (tan, tan_local)))
        for kind in range(3)
    ]
    for copy in loads:
        copy.start()
    txt_copy.start()
    cot_copy.start()

    barrier = pltpu.get_barrier_semaphore()

    def greet(i, carry):
        t = ((x + i // side) % side) * side + (y + i % side) % side
        pl.semaphore_signal(barrier, inc=1, device_id={"tensor": t}, device_id_type=MESH)
        return carry

    lax.fori_loop(1, n_t, greet, 0)

    def greet_z(i, carry):
        pl.semaphore_signal(
            barrier, inc=1, device_id={"dp": ((z + i) % n_z) * 2 + c}, device_id_type=MESH
        )
        return carry

    lax.fori_loop(1, n_z, greet_z, 0)
    pl.semaphore_signal(barrier, inc=1, device_id=twin(), device_id_type=MESH)

    for o in range(2):
        for k in range(side):
            group_weight[o, k * 256 + 192 : k * 256 + 256, :] = jnp.zeros((64, half), LOW)

    def text_rows(s):
        text_pad[320:384, :] = jnp.zeros((64, 256), LOW)
        text_pad[0:txt_len, :] = txt_local[s]
        kv = text_pad[:, 0:128].astype(F32)
        dkv = text_pad[:, 128:256].astype(F32)
        key_pair = jnp.where(low_half, kv, swap_halves(dkv))
        val_pair = jnp.where(low_half, swap_halves(kv), dkv)
        key_t = key_pair.T.astype(LOW)
        score_rhs[s, 0:64, 0:keys_pad] = jnp.zeros((64, keys_pad), LOW)
        score_rhs[s, 64:128, img:keys_pad] = key_t[0:64]
        score_rhs[s, :, keys_pad + img : 2 * keys_pad] = key_t
        value_rhs[s, img:keys_pad, :] = val_pair.astype(LOW)
        value_rhs[s, keys_pad + img : 2 * keys_pad, :] = jnp.where(low_half, 0.0, kv).astype(LOW)

    for n, local in enumerate((qkv_local, tan_local)):
        for kind in range(3):
            loads[3 * n + kind].wait()
            for page in range(width // 128):
                staged[3 * n + kind, page] = local[kind, :, page * 128 : page * 128 + 128]

    def pick(s, t):
        head = jnp.maximum(table[s, t], 0)
        page = lax.shift_right_logical(head, 1)
        odd = jnp.full((1, 128), lax.bitwise_and(head, 1), jnp.int32) == 1

        def pair(first, second):
            a = staged[first, page]
            b = staged[second, page]
            return jnp.where(
                low_half, jnp.where(odd, swap_halves(a), a), jnp.where(odd, b, swap_halves(b))
            )

        outbox[s, t, :, 0:128] = pair(3, 0) * jnp.asarray(0.125, LOW)
        outbox[s, t, :, 128:256] = pair(1, 4)
        outbox[s, t, :, 256:384] = pair(2, 5)

    pl.semaphore_wait(barrier, n_t + n_z - 1)

    def in_copy(s, t):
        return pltpu.make_async_remote_copy(
            src_ref=outbox.at[s, t],
            dst_ref=arrived.at[s, me],
            send_sem=a_send.at[s, t],
            recv_sem=a_recv.at[s, me],
            device_id={"tensor": t},
            device_id_type=MESH,
        )

    def ring(step):
        def one(i, carry):
            step(((x + i // side) % side) * side + (y + i % side) % side)
            return carry

        lax.fori_loop(1, n_t, one, 0)

    def in_own(s):
        return pltpu.make_async_copy(outbox.at[s, me], arrived.at[s, me], own_sem.at[1 + s])

    half_at = pl.multiple_of(c * offset, 128)

    chunk_rows = 2 * 192 // n_z
    chunk_cols = half // 2

    def w_span(k, at):
        return (
            pl.ds(pl.multiple_of(k * 256 + (at // 2) * chunk_rows, 16), chunk_rows),
            pl.ds(pl.multiple_of((at % 2) * chunk_cols, 128), chunk_cols),
        )

    def w_copy(k):
        return pltpu.make_async_remote_copy(
            src_ref=weight.at[
                pl.ds(pl.multiple_of((z // 2) * chunk_rows, 16), chunk_rows),
                pl.ds(pl.multiple_of(c * offset + (z % 2) * chunk_cols, 128), chunk_cols),
            ],
            dst_ref=group_weight.at[(c,) + w_span(place(c), z)],
            send_sem=w_send.at[k],
            recv_sem=w_recv.at[place(c)],
            device_id={"tensor": line(c, k)},
            device_id_type=MESH,
        )

    def w_arrival(k):
        return pltpu.make_async_remote_copy(
            src_ref=group_weight.at[(c,) + w_span(k, z)],
            dst_ref=group_weight.at[(c,) + w_span(k, z)],
            send_sem=w_send.at[k],
            recv_sem=w_recv.at[k],
            device_id={"tensor": line(c, k)},
            device_id_type=MESH,
        )

    def x_copy(k, at, way, hop):
        return pltpu.make_async_remote_copy(
            src_ref=group_weight.at[(c,) + w_span(k, at)],
            dst_ref=group_weight.at[(c,) + w_span(k, at)],
            send_sem=x_send.at[k, way, hop],
            recv_sem=x_recv.at[k, at],
            device_id={"dp": ((z + 1 - 2 * way + n_z) % n_z) * 2 + c},
            device_id_type=MESH,
        )

    reach = (n_z // 2, n_z // 2 - 1)

    def x_step(hop):
        for way in range(2):
            if hop >= 1 and hop <= reach[way]:
                at = (z + (2 * way - 1) * hop + n_z) % n_z
                for i in range(1, side):
                    k = (place(c) + i) % side
                    x_copy(k, at, way, hop % side).wait_recv()
                    if hop < reach[way]:
                        x_copy(k, at, way, hop).start()
            if hop == 0:
                for i in range(1, side):
                    x_copy((place(c) + i) % side, z, way, 0).start()

    def x_sent():
        for way in range(2):
            for hop in range(reach[way]):
                at = (z + (2 * way - 1) * hop + n_z) % n_z
                for i in range(1, side):
                    x_copy((place(c) + i) % side, at, way, hop).wait_send()

    def w_own():
        return pltpu.make_async_copy(
            weight.at[:, pl.ds(half_at, half)],
            group_weight.at[c, pl.ds(place(c) * 256, 192)],
            own_sem.at[0],
        )

    def f_copy(k):
        return pltpu.make_async_remote_copy(
            src_ref=group_weight.at[c, pl.ds(k * 256, 192)],
            dst_ref=group_weight.at[c, pl.ds(k * 256, 192)],
            send_sem=f_send.at[k],
            recv_sem=f_recv.at[k],
            device_id=twin(),
            device_id_type=MESH,
        )

    def f_arrival(k):
        return pltpu.make_async_remote_copy(
            src_ref=group_weight.at[1 - c, pl.ds(k * 256, 192)],
            dst_ref=group_weight.at[1 - c, pl.ds(k * 256, 192)],
            send_sem=f_send.at[k],
            recv_sem=f_recv.at[k],
            device_id=twin(),
            device_id_type=MESH,
        )

    w_own().start()
    for i in range(1, side):
        w_copy((place(c) + i) % side).start()

    def depart(s):
        def one(t):
            pick(s, t)
            in_copy(s, t).start()

        ring(one)

    ring(lambda t: pick(0, t))
    for i in range(1, side):
        w_arrival((place(c) + i) % side).wait_recv()
    x_step(0)
    ring(lambda t: in_copy(0, t).start())
    depart(1)
    txt_copy.wait()
    for s in range(slots):
        pick(s, me)
        in_own(s).start()
        text_rows(s)
    x_step(1)
    ring(lambda t: pick(2, t))
    x_step(2)

    def last_slot(t):
        in_copy(0, t).wait_send()
        in_copy(2, t).start()

    ring(last_slot)

    def p_copy(s, o, k, q):
        if o == 0:
            source, target = attn.at[s, q, k], regroup.at[0, s, y, q]
        else:
            source, target = attn.at[s, k], regroup.at[1, s, x]
        return pltpu.make_async_remote_copy(
            src_ref=source,
            dst_ref=target,
            send_sem=p_send.at[o, s, k, q],
            recv_sem=p_recv.at[o, s, place(o), q],
            device_id={"tensor": line(o, k)},
            device_id_type=MESH,
        )

    def p_arrival(s, o, k, q):
        target = regroup.at[0, s, k, q] if o == 0 else regroup.at[1, s, k]
        return pltpu.make_async_remote_copy(
            src_ref=target,
            dst_ref=target,
            send_sem=p_send.at[o, s, k, q],
            recv_sem=p_recv.at[o, s, k, q],
            device_id={"tensor": line(o, k)},
            device_id_type=MESH,
        )

    def one_slot(s, carry):
        def arrival(i, inner):
            t = (me + i) % n_t
            pltpu.make_async_remote_copy(
                src_ref=outbox.at[s, t],
                dst_ref=arrived.at[s, t],
                send_sem=a_send.at[s, t],
                recv_sem=a_recv.at[s, t],
                device_id={"tensor": t},
                device_id_type=MESH,
            ).wait_recv()
            return inner

        lax.fori_loop(1, n_t, arrival, 0)
        in_own(s).wait()
        key_t = arrived[s, :, :, 128:256].reshape(img, 128).astype(F32).T.astype(LOW)
        score_rhs[s, 64:128, 0:img] = key_t[0:64]
        score_rhs[s, :, keys_pad : keys_pad + img] = key_t
        val_pair = arrived[s, :, :, 256:384].reshape(img, 128)
        value_rhs[s, 0:img, :] = val_pair
        value_rhs[s, keys_pad : keys_pad + img, :] = jnp.where(
            low_half, 0.0, swap_halves(val_pair.astype(F32))
        ).astype(LOW)
        filled = jnp.where(jnp.full((1, 128), table[s, me], jnp.int32) >= 0, 1.0, 0.0)

        def one_block(turn, inner):
            q = (x + 1 + turn) % side
            lhs = arrived[s, pl.ds(q * side, side), :, 0:128].reshape(group_rows, 128)
            scores = jnp.dot(lhs, score_rhs[s, :, 0:keys_pad], preferred_element_type=F32)
            tangents = jnp.dot(
                lhs, score_rhs[s, :, keys_pad : 2 * keys_pad], preferred_element_type=F32
            )
            valid = lax.broadcasted_iota(jnp.int32, (1, 128), 1) < keys - (keys_pad - 128)
            scores = jnp.concatenate(
                [
                    scores[:, : keys_pad - 128],
                    jnp.where(valid, scores[:, keys_pad - 128 :], -1e30),
                ],
                1,
            )
            top = jnp.max(scores, axis=1, keepdims=True)
            raised = jnp.exp(scores - top)
            total = jnp.sum(raised, axis=1, keepdims=True)
            mean = jnp.sum(raised * tangents, axis=1, keepdims=True) / total
            shifted = raised * (tangents - mean)
            joined = jnp.dot(
                raised.astype(LOW), value_rhs[s, 0:keys_pad, :], preferred_element_type=F32
            ) + jnp.dot(
                shifted.astype(LOW),
                value_rhs[s, keys_pad : 2 * keys_pad, :],
                preferred_element_type=F32,
            )
            joined = (joined / total * filled).astype(LOW)
            attn[s, q] = joined.reshape(side, rows, 128)
            for i in range(1, side):
                p_copy(s, 0, (y + i) % side, q).start()

            @pl.when(turn < side - 1)
            def _():
                p_copy(s, 1, q, 0).start()

            return inner

        lax.fori_loop(0, side, one_block, 0)
        regroup[0, s, y] = attn[s, :, y]
        regroup[1, s, x] = attn[s, x]

        @pl.when(s == 0)
        def _():
            x_step(3)

        @pl.when(s == 1)
        def _():
            x_step(4)
            w_own().wait()
            for k in range(side):
                f_copy(k).start()


        return carry

    lax.fori_loop(0, slots, one_slot, 0)

    def r_copy(kind, o, j, k):
        span = pl.ds(pl.multiple_of(j * 256, 256), 256)
        return pltpu.make_async_remote_copy(
            src_ref=part_out.at[kind, o, k, :, span],
            dst_ref=part_in.at[kind, o, place(1 - o), :, span],
            send_sem=r_send.at[kind, o, j, k],
            recv_sem=r_recv.at[kind, o, j, place(1 - o)],
            device_id={"tensor": line(1 - o, k)},
            device_id_type=MESH,
        )

    def r_arrival(kind, o, j, k):
        span = pl.ds(pl.multiple_of(j * 256, 256), 256)
        return pltpu.make_async_remote_copy(
            src_ref=part_out.at[kind, o, k, :, span],
            dst_ref=part_in.at[kind, o, k, :, span],
            send_sem=r_send.at[kind, o, j, k],
            recv_sem=r_recv.at[kind, o, j, k],
            device_id={"tensor": line(1 - o, k)},
            device_id_type=MESH,
        )

    for o in range(2):
        for s in range(slots):
            for i in range(1, side):
                k = (place(o) + i) % side
                for q in range(side if o == 0 else 1):
                    p_arrival(s, o, k, q).wait_recv()

        def tangents_of(k, carry, o=o):
            first = regroup[o, 0, k].reshape(group_rows, 128).astype(F32)
            second = regroup[o, 1, k].reshape(group_rows, 128).astype(F32)
            third = regroup[o, 2, k].reshape(group_rows, 128).astype(F32)
            tang = jnp.where(low_half, swap_halves(first), second)
            tang_last = jnp.where(low_half, swap_halves(third), 0.0)
            at = pl.multiple_of(k * 256, 256)
            proj_lhs[1, o, :, pl.ds(at, 128)] = tang.astype(LOW)
            proj_lhs[1, o, :, pl.ds(at + 128, 128)] = tang_last.astype(LOW)
            return carry

        lax.fori_loop(0, side, tangents_of, 0)

    for k in range(side):
        f_arrival(k).wait_recv()

    steps = half // 256

    def project(kind):
        def one(n, carry):
            o = n % 2
            j = n // 2
            span = pl.ds(pl.multiple_of(j * 256, 256), 256)
            part = jnp.dot(
                proj_lhs[kind, o], group_weight[o, :, span], preferred_element_type=F32
            ).astype(LOW)
            for k in range(side):
                part_out[kind, o, k, :, span] = part[k * rows : (k + 1) * rows]
            own = place(1 - o)
            for i in range(1, side):
                r_copy(kind, o, j, (own + i) % side).start()
            part_in[kind, o, own, :, span] = part_out[kind, o, own, :, span]
            return carry

        lax.fori_loop(0, 2 * steps, one, 0)

    def gathered(kind):
        def one(n, carry):
            for i in range(1, side):
                r_arrival(kind, n % 2, n // 2, (place(1 - n % 2) + i) % side).wait_recv()
            return carry

        lax.fori_loop(0, 2 * steps, one, 0)

    project(1)

    for o in range(2):

        def prims_of(k, carry, o=o):
            first = regroup[o, 0, k].reshape(group_rows, 128).astype(F32)
            second = regroup[o, 1, k].reshape(group_rows, 128).astype(F32)
            third = regroup[o, 2, k].reshape(group_rows, 128).astype(F32)
            prim = jnp.where(low_half, first, swap_halves(second))
            prim_last = jnp.where(low_half, third, 0.0)
            at = pl.multiple_of(k * 256, 256)
            proj_lhs[0, o, :, pl.ds(at, 128)] = prim.astype(LOW)
            proj_lhs[0, o, :, pl.ds(at + 128, 128)] = prim_last.astype(LOW)
            prim_t[o, k, 0:128, :] = prim.T.astype(LOW)
            prim_t[o, k, 128:192, :] = prim_last.T[0:64].astype(LOW)
            return carry

        lax.fori_loop(0, side, prims_of, 0)

    skip = 2 * half - width

    def collect(kind, o, first, last):
        total = part_in[kind, o, 0, :, first:last].astype(F32)
        for k in range(1, side):
            total = total + part_in[kind, o, k, :, first:last].astype(F32)
        return total

    own_squares = jnp.zeros((1, 128), F32)
    for n in range(2 * steps):
        o, j = n % 2, n // 2
        for i in range(1, side):
            r_arrival(1, o, j, (place(1 - o) + i) % side).wait_recv()
        first = max(j * 256, skip * o)
        columns = collect(1, o, first, j * 256 + 256)
        at = o * offset + first
        tan_sum[:, at : at + columns.shape[1]] = columns
        column_squares = jnp.sum(columns * columns, axis=0, keepdims=True)
        for lane in range(0, columns.shape[1], 128):
            own_squares = own_squares + column_squares[:, lane : lane + 128]
    squares[me] = jnp.broadcast_to(jnp.sum(own_squares, axis=1, keepdims=True), (8, 128))

    def q_copy(t):
        return pltpu.make_async_remote_copy(
            src_ref=squares.at[me],
            dst_ref=squares.at[me],
            send_sem=q_send.at[t],
            recv_sem=q_recv.at[me],
            device_id={"tensor": t},
            device_id_type=MESH,
        )

    def q_start(i, carry):
        q_copy((me + i) % n_t).start()
        return carry

    lax.fori_loop(1, n_t, q_start, 0)
    def q_wait(i, carry):
        t = (me + i) % n_t
        pltpu.make_async_remote_copy(
            src_ref=squares.at[t],
            dst_ref=squares.at[t],
            send_sem=q_send.at[t],
            recv_sem=q_recv.at[t],
            device_id={"tensor": t},
            device_id_type=MESH,
        ).wait_recv()
        return carry

    lax.fori_loop(1, n_t, q_wait, 0)
    square_sum = jnp.sum(squares[...], axis=0)[0:1, 0:1]
    divisor = jnp.sqrt(square_sum / (img * width)) + 0.1
    normal = (tan_sum[...] / divisor).astype(LOW)
    tangent_out[...] = normal
    cot_copy.wait()
    upstream[...] = (cot_local[...].astype(F32) - normal.astype(F32)).astype(LOW)

    starts = (0, 384, 640, 1024)
    sizes = (384, 256, 384, 256)

    def cut(p):
        return pl.ds(starts[p], sizes[p])

    def u_copy(o, p, k):
        return pltpu.make_async_remote_copy(
            src_ref=upstream.at[:, pl.ds(o * offset + starts[p], sizes[p])],
            dst_ref=up_all.at[o, pl.ds(place(1 - o) * rows, rows), cut(p)],
            send_sem=u_send.at[o, p, k],
            recv_sem=u_recv.at[o, p, place(1 - o)],
            device_id={"tensor": line(1 - o, k)},
            device_id_type=MESH,
        )

    def u_arrival(o, p, k):
        return pltpu.make_async_remote_copy(
            src_ref=up_all.at[o, pl.ds(k * rows, rows), cut(p)],
            dst_ref=up_all.at[o, pl.ds(k * rows, rows), cut(p)],
            send_sem=u_send.at[o, p, k],
            recv_sem=u_recv.at[o, p, k],
            device_id={"tensor": line(1 - o, k)},
            device_id_type=MESH,
        )

    def up_leaves(p):
        for i in range(1, side):
            for o in range(2):
                k = (place(1 - o) + i) % side
                if p > 0:
                    u_copy(o, p - 1, k).wait_send()
                u_copy(o, p, k).start()

    up_leaves(0)
    for o in range(2):
        up_all[o, pl.ds(place(1 - o) * rows, rows), :] = upstream[:, o * offset : o * offset + half]
    up_leaves(1)

    def t_copy(p, k):
        return pltpu.make_async_remote_copy(
            src_ref=twin_out.at[k, :, cut(p)],
            dst_ref=twin_in.at[k, :, cut(p)],
            send_sem=t_send.at[p, k],
            recv_sem=t_recv.at[p, k],
            device_id=twin(),
            device_id_type=MESH,
        )

    def g_copy(p, k):
        return pltpu.make_async_remote_copy(
            src_ref=grad_send.at[k, :, cut(p)],
            dst_ref=grad_in.at[place(c), :, cut(p)],
            send_sem=g_send.at[p, k],
            recv_sem=g_recv.at[p, place(c)],
            device_id={"tensor": line(c, k)},
            device_id_type=MESH,
        )

    def g_arrival(p, k):
        return pltpu.make_async_remote_copy(
            src_ref=grad_in.at[k, :, cut(p)],
            dst_ref=grad_in.at[k, :, cut(p)],
            send_sem=g_send.at[p, k],
            recv_sem=g_recv.at[p, k],
            device_id={"tensor": line(c, k)},
            device_id_type=MESH,
        )

    own = place(c)

    def grad_part(p):
        for o in range(2):
            for i in range(1, side):
                u_arrival(o, p, (place(1 - o) + i) % side).wait_recv()
        if p + 2 < 4:
            up_leaves(p + 2)

        def for_twin(i, inner):
            k = (own + i) % side
            twin_out[k, :, cut(p)] = jnp.dot(
                prim_t[1 - c, k], up_all[1 - c, :, cut(p)], preferred_element_type=F32
            ).astype(LOW)
            t_copy(p, k).start()
            return inner

        lax.fori_loop(1, side + 1, for_twin, 0)

        def for_line(i, inner):
            k = (own + i) % side
            mine = jnp.dot(prim_t[c, k], up_all[c, :, cut(p)], preferred_element_type=F32)
            t_copy(p, k).wait_recv()
            grad_send[k, :, cut(p)] = (mine + twin_in[k, :, cut(p)].astype(F32)).astype(LOW)

            @pl.when(i < side)
            def _():
                if p > 0:
                    g_copy(p - 1, k).wait_send()
                g_copy(p, k).start()

            return inner

        lax.fori_loop(1, side + 1, for_line, 0)
        grad_in[own, :, cut(p)] = grad_send[own, :, cut(p)]

    def chunk(k):
        return (
            pl.ds(pl.multiple_of((k // 2) * chunk_rows, 16), chunk_rows),
            pl.ds(pl.multiple_of((k % 2) * chunk_cols, 128), chunk_cols),
        )

    def z_copy(p, k, source):
        inner = pl.ds(starts[p] % chunk_cols, sizes[p])
        return pltpu.make_async_remote_copy(
            src_ref=z_out.at[pl.ds(pl.multiple_of((k // 2) * chunk_rows, 16), chunk_rows), cut(p)],
            dst_ref=z_in.at[source, :, inner],
            send_sem=z_send.at[p, k],
            recv_sem=z_recv.at[p % 2, source],
            device_id={"dp": k * 2 + c},
            device_id_type=MESH,
        )

    def c_copy(k, owner):
        return pltpu.make_async_remote_copy(
            src_ref=final.at[(c,) + chunk(owner)],
            dst_ref=final.at[(c,) + chunk(owner)],
            send_sem=c_send.at[k],
            recv_sem=c_recv.at[owner],
            device_id={"dp": k * 2 + c},
            device_id_type=MESH,
        )

    def z_loop(step):
        def one(i, carry):
            step((z + i) % n_z)
            return carry

        lax.fori_loop(1, n_z, one, 0)

    def z_part(p, step):
        def one(i, inner):
            k = (z + i) % n_z

            @pl.when(k % 2 == p // 2)
            def _():
                step(k)

            return inner

        lax.fori_loop(1, n_z, one, 0)

    def to_owners(p):
        for i in range(1, side):
            g_arrival(p, (own + i) % side).wait_recv()
        total = grad_in[0, :, cut(p)].astype(F32)
        for k in range(1, side):
            total = total + grad_in[k, :, cut(p)].astype(F32)
        z_out[:, cut(p)] = total.astype(LOW)
        z_part(p, lambda k: z_copy(p, k, z).start())

    grad_part(0)
    grad_part(1)
    to_owners(0)
    grad_part(2)
    to_owners(1)
    grad_part(3)
    to_owners(2)
    to_owners(3)

    z_in[z] = z_out[chunk(z)]
    z_loop(lambda k: z_copy(0, k, k).wait_recv())
    z_loop(lambda k: z_copy(1, k, k).wait_recv())
    total = z_in[0].astype(F32)
    for k in range(1, n_z):
        total = total + z_in[k].astype(F32)
    final[(c,) + chunk(z)] = (total * (1.0 / (2 * n_z))).astype(LOW)
    z_loop(lambda k: c_copy(k, z).start())
    project(0)
    gathered(0)
    image_out[:, 0:half] = collect(0, 0, 0, half).astype(LOW)
    image_out[:, half:width] = collect(0, 1, skip, half).astype(LOW)
    z_loop(lambda k: c_copy(k, k).wait_recv())

    def s_copy(which):
        return pltpu.make_async_remote_copy(
            src_ref=final.at[which],
            dst_ref=final.at[which],
            send_sem=s_send,
            recv_sem=s_recv,
            device_id=twin(),
            device_id_type=MESH,
        )

    s_copy(c).start()

    ring(lambda t: in_copy(1, t).wait_send())
    ring(lambda t: in_copy(2, t).wait_send())
    x_sent()
    for i in range(1, side):
        w_copy((place(c) + i) % side).wait_send()
        for o in range(2):
            for s in range(slots):
                for q in range(side if o == 0 else 1):
                    p_copy(s, o, (place(o) + i) % side, q).wait_send()
            u_copy(o, 3, (place(1 - o) + i) % side).wait_send()
        g_copy(3, (place(c) + i) % side).wait_send()

    def r_sent(n, carry):
        o = n % 2
        for kind in range(2):
            for i in range(1, side):
                r_copy(kind, o, n // 2, (place(1 - o) + i) % side).wait_send()
        return carry

    lax.fori_loop(0, 2 * steps, r_sent, 0)
    for k in range(side):
        f_copy(k).wait_send()
        for p in range(4):
            t_copy(p, k).wait_send()

    def q_sent(i, carry):
        q_copy((me + i) % n_t).wait_send()
        return carry

    lax.fori_loop(1, n_t, q_sent, 0)
    for p in range(4):
        z_part(p, lambda k, p=p: z_copy(p, k, z).wait_send())
    z_loop(lambda k: c_copy(k, z).wait_send())
    s_copy(c).wait_send()
    s_copy(1 - c).wait_recv()
    grad_out[...] = final[...]


def on_device(n_t, n_dp, qkv_img, tan_img, txt_kv, head_table, out_weight, cotangent):
    rows, width = qkv_img.shape[1], qkv_img.shape[3]
    slots = head_table.shape[1]
    side = 4
    n_z = n_dp // 2
    txt_len = txt_kv.shape[2]
    img = n_t * rows
    keys = img + txt_len
    keys_pad = -(-keys // 128) * 128
    half = -(-width // 256) * 128
    offset = width - half
    dims = (n_t, side, n_z, slots, rows, keys, keys_pad, half, offset, width, txt_len)
    dma = pltpu.SemaphoreType.DMA
    vmem = pl.BlockSpec(memory_space=pltpu.VMEM)
    hbm = pl.BlockSpec(memory_space=pl.ANY)
    steps = half // 256
    image, tangent, grad = pl.pallas_call(
        functools.partial(body, dims),
        out_shape=(
            jax.ShapeDtypeStruct((rows, width), LOW),
            jax.ShapeDtypeStruct((rows, width), LOW),
            jax.ShapeDtypeStruct((2, 192, half), LOW),
        ),
        in_specs=[pl.BlockSpec(memory_space=pltpu.SMEM)] + [hbm] * 5,
        out_specs=(vmem, vmem, vmem),
        scratch_shapes=[
            pltpu.VMEM((rows, width), LOW),
            pltpu.VMEM((3, rows, width), LOW),
            pltpu.VMEM((3, rows, width), LOW),
            pltpu.VMEM((slots, txt_len, 256), LOW),
            pltpu.VMEM((6, width // 128, rows, 128), LOW),
            pltpu.VMEM((slots, n_t, rows, 384), LOW),
            pltpu.VMEM((slots, n_t, rows, 384), LOW),
            pltpu.VMEM((384, 256), LOW),
            pltpu.VMEM((slots, 128, 2 * keys_pad), LOW),
            pltpu.VMEM((slots, 2 * keys_pad, 128), LOW),
            pltpu.VMEM((slots, side, side, rows, 128), LOW),
            pltpu.VMEM((2, slots, side, side, rows, 128), LOW),
            pltpu.VMEM((2, side * 256, half), LOW),
            pltpu.VMEM((2, 2, side * rows, side * 256), LOW),
            pltpu.VMEM((2, side, 192, side * rows), LOW),
            pltpu.VMEM((2, 2, side, rows, half), LOW),
            pltpu.VMEM((2, 2, side, rows, half), LOW),
            pltpu.VMEM((rows, width), F32),
            pltpu.VMEM((n_t, 8, 128), F32),
            pltpu.VMEM((rows, width), LOW),
            pltpu.VMEM((2, side * rows, half), LOW),
            pltpu.VMEM((side, 192, half), LOW),
            pltpu.VMEM((side, 192, half), LOW),
            pltpu.VMEM((side, 192, half), LOW),
            pltpu.VMEM((side, 192, half), LOW),
            pltpu.VMEM((192, half), LOW),
            pltpu.VMEM((n_z, 2 * 192 // n_z, half // 2), LOW),
            pltpu.VMEM((2, 192, half), LOW),
            dma((slots, n_t)),
            dma((slots, n_t)),
            dma((side,)),
            dma((side,)),
            dma((side, 2, n_z // 2)),
            dma((side, n_z)),
            dma((side,)),
            dma((side,)),
            dma((9 + slots,)),
            dma((2, slots, side, side)),
            dma((2, slots, side, side)),
            dma((2, 2, steps, side)),
            dma((2, 2, steps, side)),
            dma((n_t,)),
            dma((n_t,)),
            dma((2, 4, side)),
            dma((2, 4, side)),
            dma((4, side)),
            dma((4, side)),
            dma((4, side)),
            dma((4, side)),
            dma((4, n_z)),
            dma((2, n_z)),
            dma((n_z,)),
            dma((n_z,)),
            dma,
            dma,
        ],
        compiler_params=pltpu.CompilerParams(
            collective_id=0, has_side_effects=True, vmem_limit_bytes=56 * 1024 * 1024
        ),
    )(
        head_table.T,
        jnp.transpose(qkv_img[0], (1, 0, 2)),
        jnp.transpose(tan_img[0], (1, 0, 2)),
        txt_kv[0],
        out_weight,
        cotangent[0],
    )
    return pl.pallas_call(
        finish,
        out_shape=(
            jax.ShapeDtypeStruct((rows, width), LOW),
            jax.ShapeDtypeStruct((rows, width), LOW),
            jax.ShapeDtypeStruct((slots * 64, width), F32),
        ),
        in_specs=[hbm, hbm, hbm],
        out_specs=(hbm, hbm, hbm),
        scratch_shapes=[
            pltpu.VMEM((2, rows, width), LOW),
            pltpu.VMEM((2, 192, half), LOW),
            pltpu.VMEM((192, width), F32),
            dma((4,)),
            dma((4,)),
            dma((4,)),
        ],
    )(image, tangent, grad)


def solution(mesh):
    n_t, n_dp = mesh.shape["tensor"], mesh.shape["dp"]

    def step(*args):
        image_out, tangent_out, weight_grad = on_device(n_t, n_dp, *args)
        return image_out[None], tangent_out[None], weight_grad

    return jax.shard_map(
        step,
        mesh=mesh,
        in_specs=(
            P("dp", "tensor", None, None),
            P("dp", "tensor", None, None),
            P("dp", "tensor", None, None),
            P(),
            P("tensor", None),
            P("dp", "tensor", None),
        ),
        out_specs=(P("dp", "tensor", None), P("dp", "tensor", None), P("tensor", None)),
        check_vma=False,
    )
```

```python
import functools

import jax
import jax.numpy as jnp
from jax import lax
from jax.experimental import pallas as pl
from jax.experimental.pallas import tpu as pltpu
from jax.sharding import PartitionSpec as P

MESH = pl.DeviceIdType.MESH
F32 = jnp.float32
LOW = jnp.bfloat16


def swap_halves(value):
    return pltpu.roll(value, 64, 1)


def finish(
    image, tangent, grad, image_out, tangent_out, grad_out, pair, held, wide, in_sem, out_sem, way_sem
):
    half = grad.shape[2]
    width = image.shape[1]
    skip = 2 * half - width
    blocks = 4
    tall = grad.shape[1] // blocks

    def load(i):
        rows = pl.ds(i * tall, tall)
        return pltpu.make_async_copy(grad.at[:, rows], held.at[:, rows], in_sem.at[i])

    def store(i):
        rows = pl.ds(i * tall, tall)
        return pltpu.make_async_copy(wide.at[rows], grad_out.at[rows], out_sem.at[i])

    for i in range(blocks):
        load(i).start()
    there = (
        pltpu.make_async_copy(image, pair.at[0], way_sem.at[0]),
        pltpu.make_async_copy(tangent, pair.at[1], way_sem.at[1]),
    )
    back = (
        pltpu.make_async_copy(pair.at[0], image_out, way_sem.at[2]),
        pltpu.make_async_copy(pair.at[1], tangent_out, way_sem.at[3]),
    )
    for copy in there:
        copy.start()
    for i in range(blocks):
        load(i).wait()
        rows = pl.ds(i * tall, tall)
        wide[rows, 0:half] = held[0, rows].astype(F32)
        wide[rows, half:width] = held[1, rows, skip:].astype(F32)
        store(i).start()
    for copy, after in zip(there, back):
        copy.wait()
        after.start()
    for i in range(blocks):
        store(i).wait()
    for copy in back:
        copy.wait()


def body(
    dims,
    table,
    qkv,
    tan,
    txt,
    weight,
    cot,
    image_out,
    tangent_out,
    grad_out,
    cot_local,
    qkv_local,
    tan_local,
    txt_local,
    staged,
    outbox,
    arrived,
    text_pad,
    score_rhs,
    value_rhs,
    attn,
    regroup,
    group_weight,
    proj_lhs,
    prim_t,
    part_out,
    part_in,
    tan_sum,
    squares,
    upstream_a,
    upstream_b,
    up_all_a,
    up_all_b,
    prim_in,
    grad_send_a,
    grad_send_b,
    grad_in_a,
    grad_in_b,
    z_out_a,
    z_out_b,
    z_in_a,
    z_in_b,
    final_a,
    final_b,
    a_send,
    a_recv,
    w_send,
    w_recv,
    x_send,
    x_recv,
    f_send,
    f_recv,
    own_sem,
    p_send,
    p_recv,
    r_send,
    r_recv,
    q_send,
    q_recv,
    u_send,
    u_recv,
    t_send,
    t_recv,
    g_send,
    g_recv,
    z_send,
    z_recv,
    c_send,
    c_recv,
    s_send,
    s_recv,
):
    n_t, side, n_z, slots, rows, keys, keys_pad, half, offset, width, txt_len = dims
    me = lax.axis_index("tensor")
    dp = lax.axis_index("dp")
    x = me // side
    y = me % side
    z = dp // 2
    c = dp % 2
    upstream = (upstream_a, upstream_b)
    up_all = (up_all_a, up_all_b)
    grad_send = (grad_send_a, grad_send_b)
    grad_in = (grad_in_a, grad_in_b)
    z_out = (z_out_a, z_out_b)
    z_in = (z_in_a, z_in_b)
    final = (final_a, final_b)
    img = n_t * rows
    group_rows = side * rows

    def line(o, k):
        return (1 - o) * (x * side + k) + o * (k * side + y)

    def place(o):
        return (1 - o) * y + o * x

    def twin():
        return {"dp": z * 2 + (1 - c)}

    low_half = lax.broadcasted_iota(jnp.int32, (1, 128), 1) < 64

    cot_copy = pltpu.make_async_copy(cot, cot_local, own_sem.at[1 + slots])
    txt_copy = pltpu.make_async_copy(txt, txt_local, own_sem.at[2 + slots])
    loads = [
        pltpu.make_async_copy(whole.at[kind], local.at[kind], own_sem.at[3 + slots + 3 * n + kind])
        for n, (whole, local) in enumerate(((qkv, qkv_local), (tan, tan_local)))
        for kind in range(3)
    ]
    for copy in loads:
        copy.start()
    txt_copy.start()
    cot_copy.start()

    barrier = pltpu.get_barrier_semaphore()

    def greet(i, carry):
        t = ((x + i // side) % side) * side + (y + i % side) % side
        pl.semaphore_signal(barrier, inc=1, device_id={"tensor": t}, device_id_type=MESH)
        return carry

    lax.fori_loop(1, n_t, greet, 0)

    def greet_z(i, carry):
        pl.semaphore_signal(
            barrier, inc=1, device_id={"dp": ((z + i) % n_z) * 2 + c}, device_id_type=MESH
        )
        return carry

    lax.fori_loop(1, n_z, greet_z, 0)
    pl.semaphore_signal(barrier, inc=1, device_id=twin(), device_id_type=MESH)
    for o in range(2):
        for i in range(1, side):
            pl.semaphore_signal(
                barrier,
                inc=1,
                device_id={"tensor": line(o, (place(o) + i) % side), "dp": z * 2 + (1 - c)},
                device_id_type=MESH,
            )

    for o in range(2):
        for k in range(side):
            group_weight[o, k * 256 + 192 : k * 256 + 256, :] = jnp.zeros((64, half), LOW)

    def text_rows(s):
        text_pad[320:384, :] = jnp.zeros((64, 256), LOW)
        text_pad[0:txt_len, :] = txt_local[s]
        kv = text_pad[:, 0:128].astype(F32)
        dkv = text_pad[:, 128:256].astype(F32)
        key_pair = jnp.where(low_half, kv, swap_halves(dkv))
        val_pair = jnp.where(low_half, swap_halves(kv), dkv)
        key_t = key_pair.T.astype(LOW)
        score_rhs[s, 0:64, 0:keys_pad] = jnp.zeros((64, keys_pad), LOW)
        score_rhs[s, 64:128, img:keys_pad] = key_t[0:64]
        score_rhs[s, :, keys_pad + img : 2 * keys_pad] = key_t
        value_rhs[s, img:keys_pad, :] = val_pair.astype(LOW)
        value_rhs[s, keys_pad + img : 2 * keys_pad, :] = jnp.where(low_half, 0.0, kv).astype(LOW)

    for n, local in enumerate((qkv_local, tan_local)):
        for kind in range(3):
            loads[3 * n + kind].wait()
            for page in range(width // 128):
                staged[3 * n + kind, page] = local[kind, :, page * 128 : page * 128 + 128]

    def pick(s, t):
        head = jnp.maximum(table[s, t], 0)
        page = lax.shift_right_logical(head, 1)
        odd = jnp.full((1, 128), lax.bitwise_and(head, 1), jnp.int32) == 1

        def pair(first, second):
            a = staged[first, page]
            b = staged[second, page]
            return jnp.where(
                low_half, jnp.where(odd, swap_halves(a), a), jnp.where(odd, b, swap_halves(b))
            )

        outbox[s, t, :, 0:128] = pair(3, 0) * jnp.asarray(0.125, LOW)
        outbox[s, t, :, 128:256] = pair(1, 4)
        outbox[s, t, :, 256:384] = pair(2, 5)

    pl.semaphore_wait(barrier, n_t + n_z - 1 + 2 * (side - 1))

    def in_copy(s, t):
        return pltpu.make_async_remote_copy(
            src_ref=outbox.at[s, t],
            dst_ref=arrived.at[s, me],
            send_sem=a_send.at[s, t],
            recv_sem=a_recv.at[s, me],
            device_id={"tensor": t},
            device_id_type=MESH,
        )

    def ring(step):
        def one(i, carry):
            step(((x + i // side) % side) * side + (y + i % side) % side)
            return carry

        lax.fori_loop(1, n_t, one, 0)

    def in_own(s):
        return pltpu.make_async_copy(outbox.at[s, me], arrived.at[s, me], own_sem.at[1 + s])

    half_at = pl.multiple_of(c * offset, 128)

    chunk_rows = 2 * 192 // n_z
    chunk_cols = half // 2

    def w_span(k, at):
        return (
            pl.ds(pl.multiple_of(k * 256 + (at // 2) * chunk_rows, 16), chunk_rows),
            pl.ds(pl.multiple_of((at % 2) * chunk_cols, 128), chunk_cols),
        )

    def w_copy(k):
        return pltpu.make_async_remote_copy(
            src_ref=weight.at[
                pl.ds(pl.multiple_of((z // 2) * chunk_rows, 16), chunk_rows),
                pl.ds(pl.multiple_of(c * offset + (z % 2) * chunk_cols, 128), chunk_cols),
            ],
            dst_ref=group_weight.at[(c,) + w_span(place(c), z)],
            send_sem=w_send.at[k],
            recv_sem=w_recv.at[place(c)],
            device_id={"tensor": line(c, k)},
            device_id_type=MESH,
        )

    def w_arrival(k):
        return pltpu.make_async_remote_copy(
            src_ref=group_weight.at[(c,) + w_span(k, z)],
            dst_ref=group_weight.at[(c,) + w_span(k, z)],
            send_sem=w_send.at[k],
            recv_sem=w_recv.at[k],
            device_id={"tensor": line(c, k)},
            device_id_type=MESH,
        )

    def x_copy(k, at, way, hop):
        return pltpu.make_async_remote_copy(
            src_ref=group_weight.at[(c,) + w_span(k, at)],
            dst_ref=group_weight.at[(c,) + w_span(k, at)],
            send_sem=x_send.at[k, way, hop],
            recv_sem=x_recv.at[k, at],
            device_id={"dp": ((z + 1 - 2 * way + n_z) % n_z) * 2 + c},
            device_id_type=MESH,
        )

    reach = (n_z // 2, n_z // 2 - 1)

    def x_step(hop):
        for way in range(2):
            if hop >= 1 and hop <= reach[way]:
                at = (z + (2 * way - 1) * hop + n_z) % n_z
                for i in range(1, side):
                    k = (place(c) + i) % side
                    x_copy(k, at, way, hop % side).wait_recv()
                    if hop < reach[way]:
                        x_copy(k, at, way, hop).start()
            if hop == 0:
                for i in range(1, side):
                    x_copy((place(c) + i) % side, z, way, 0).start()

    def x_sent():
        for way in range(2):
            for hop in range(reach[way]):
                at = (z + (2 * way - 1) * hop + n_z) % n_z
                for i in range(1, side):
                    x_copy((place(c) + i) % side, at, way, hop).wait_send()

    def w_own():
        return pltpu.make_async_copy(
            weight.at[:, pl.ds(half_at, half)],
            group_weight.at[c, pl.ds(place(c) * 256, 192)],
            own_sem.at[0],
        )

    def f_copy(k):
        return pltpu.make_async_remote_copy(
            src_ref=group_weight.at[c, pl.ds(k * 256, 192)],
            dst_ref=group_weight.at[c, pl.ds(k * 256, 192)],
            send_sem=f_send.at[k],
            recv_sem=f_recv.at[k],
            device_id=twin(),
            device_id_type=MESH,
        )

    def f_arrival(k):
        return pltpu.make_async_remote_copy(
            src_ref=group_weight.at[1 - c, pl.ds(k * 256, 192)],
            dst_ref=group_weight.at[1 - c, pl.ds(k * 256, 192)],
            send_sem=f_send.at[k],
            recv_sem=f_recv.at[k],
            device_id=twin(),
            device_id_type=MESH,
        )

    w_own().start()
    for i in range(1, side):
        w_copy((place(c) + i) % side).start()

    def depart(s):
        def one(t):
            pick(s, t)
            in_copy(s, t).start()

        ring(one)

    ring(lambda t: pick(0, t))
    for i in range(1, side):
        w_arrival((place(c) + i) % side).wait_recv()
    x_step(0)
    ring(lambda t: in_copy(0, t).start())
    depart(1)
    txt_copy.wait()
    for s in range(slots):
        pick(s, me)
        in_own(s).start()
        text_rows(s)
    x_step(1)
    ring(lambda t: pick(2, t))
    x_step(2)

    def last_slot(t):
        in_copy(0, t).wait_send()
        in_copy(2, t).start()

    ring(last_slot)

    def p_copy(s, o, k, q):
        if o == 0:
            source, target = attn.at[s, q, k], regroup.at[0, s, y, q]
        else:
            source, target = attn.at[s, k], regroup.at[1, s, x]
        return pltpu.make_async_remote_copy(
            src_ref=source,
            dst_ref=target,
            send_sem=p_send.at[o, s, k, q],
            recv_sem=p_recv.at[o, s, place(o), q],
            device_id={"tensor": line(o, k)},
            device_id_type=MESH,
        )

    def p_arrival(s, o, k, q):
        target = regroup.at[0, s, k, q] if o == 0 else regroup.at[1, s, k]
        return pltpu.make_async_remote_copy(
            src_ref=target,
            dst_ref=target,
            send_sem=p_send.at[o, s, k, q],
            recv_sem=p_recv.at[o, s, k, q],
            device_id={"tensor": line(o, k)},
            device_id_type=MESH,
        )

    def one_slot(s, carry):
        def arrival(i, inner):
            t = (me + i) % n_t
            pltpu.make_async_remote_copy(
                src_ref=outbox.at[s, t],
                dst_ref=arrived.at[s, t],
                send_sem=a_send.at[s, t],
                recv_sem=a_recv.at[s, t],
                device_id={"tensor": t},
                device_id_type=MESH,
            ).wait_recv()
            return inner

        lax.fori_loop(1, n_t, arrival, 0)
        in_own(s).wait()
        key_t = arrived[s, :, :, 128:256].reshape(img, 128).astype(F32).T.astype(LOW)
        score_rhs[s, 64:128, 0:img] = key_t[0:64]
        score_rhs[s, :, keys_pad : keys_pad + img] = key_t
        val_pair = arrived[s, :, :, 256:384].reshape(img, 128)
        value_rhs[s, 0:img, :] = val_pair
        value_rhs[s, keys_pad : keys_pad + img, :] = jnp.where(
            low_half, 0.0, swap_halves(val_pair.astype(F32))
        ).astype(LOW)
        filled = jnp.where(jnp.full((1, 128), table[s, me], jnp.int32) >= 0, 1.0, 0.0)

        def one_block(turn, inner):
            q = (x + 1 + turn) % side
            lhs = arrived[s, pl.ds(q * side, side), :, 0:128].reshape(group_rows, 128)
            scores = jnp.dot(lhs, score_rhs[s, :, 0:keys_pad], preferred_element_type=F32)
            tangents = jnp.dot(
                lhs, score_rhs[s, :, keys_pad : 2 * keys_pad], preferred_element_type=F32
            )
            valid = lax.broadcasted_iota(jnp.int32, (1, 128), 1) < keys - (keys_pad - 128)
            scores = jnp.concatenate(
                [
                    scores[:, : keys_pad - 128],
                    jnp.where(valid, scores[:, keys_pad - 128 :], -1e30),
                ],
                1,
            )
            top = jnp.max(scores, axis=1, keepdims=True)
            raised = jnp.exp(scores - top)
            total = jnp.sum(raised, axis=1, keepdims=True)
            mean = jnp.sum(raised * tangents, axis=1, keepdims=True) / total
            shifted = raised * (tangents - mean)
            joined = jnp.dot(
                raised.astype(LOW), value_rhs[s, 0:keys_pad, :], preferred_element_type=F32
            ) + jnp.dot(
                shifted.astype(LOW),
                value_rhs[s, keys_pad : 2 * keys_pad, :],
                preferred_element_type=F32,
            )
            joined = (joined / total * filled).astype(LOW)
            attn[s, q] = joined.reshape(side, rows, 128)
            for i in range(1, side):
                p_copy(s, 0, (y + i) % side, q).start()

            @pl.when(turn < side - 1)
            def _():
                p_copy(s, 1, q, 0).start()

            return inner

        lax.fori_loop(0, side, one_block, 0)
        regroup[0, s, y] = attn[s, :, y]
        regroup[1, s, x] = attn[s, x]

        @pl.when(s == 0)
        def _():
            x_step(3)

        @pl.when(s == 1)
        def _():
            x_step(4)
            w_own().wait()
            for k in range(side):
                f_copy(k).start()


        return carry

    lax.fori_loop(0, slots, one_slot, 0)

    steps = 2
    wide = half // steps

    def r_copy(kind, o, j, k):
        return pltpu.make_async_remote_copy(
            src_ref=part_out.at[kind, o, j, k],
            dst_ref=part_in.at[kind, o, j, place(1 - o)],
            send_sem=r_send.at[kind, o, j, k],
            recv_sem=r_recv.at[kind, o, j, place(1 - o)],
            device_id={"tensor": line(1 - o, k)},
            device_id_type=MESH,
        )

    def r_arrival(kind, o, j, k):
        return pltpu.make_async_remote_copy(
            src_ref=part_out.at[kind, o, j, k],
            dst_ref=part_in.at[kind, o, j, k],
            send_sem=r_send.at[kind, o, j, k],
            recv_sem=r_recv.at[kind, o, j, k],
            device_id={"tensor": line(1 - o, k)},
            device_id_type=MESH,
        )

    for o in range(2):
        for s in range(slots):
            for i in range(1, side):
                k = (place(o) + i) % side
                for q in range(side if o == 0 else 1):
                    p_arrival(s, o, k, q).wait_recv()

        def tangents_of(k, carry, o=o):
            first = regroup[o, 0, k].reshape(group_rows, 128).astype(F32)
            second = regroup[o, 1, k].reshape(group_rows, 128).astype(F32)
            third = regroup[o, 2, k].reshape(group_rows, 128).astype(F32)
            tang = jnp.where(low_half, swap_halves(first), second)
            tang_last = jnp.where(low_half, swap_halves(third), 0.0)
            at = pl.multiple_of(k * 256, 256)
            proj_lhs[1, o, :, pl.ds(at, 128)] = tang.astype(LOW)
            proj_lhs[1, o, :, pl.ds(at + 128, 128)] = tang_last.astype(LOW)
            return carry

        lax.fori_loop(0, side, tangents_of, 0)

    for k in range(side):
        f_arrival(k).wait_recv()

    def project(kind):
        def one(n, carry):
            o = n % 2
            j = n // 2
            span = pl.ds(pl.multiple_of(j * wide, 128), wide)
            part = jnp.dot(
                proj_lhs[kind, o], group_weight[o, :, span], preferred_element_type=F32
            ).astype(LOW)
            for k in range(side):
                part_out[kind, o, j, k] = part[k * rows : (k + 1) * rows]
            own = place(1 - o)
            for i in range(1, side):
                r_copy(kind, o, j, (own + i) % side).start()
            part_in[kind, o, j, own] = part_out[kind, o, j, own]
            return carry

        lax.fori_loop(0, 2 * steps, one, 0)

    def gathered(kind):
        def one(n, carry):
            for i in range(1, side):
                r_arrival(kind, n % 2, n // 2, (place(1 - n % 2) + i) % side).wait_recv()
            return carry

        lax.fori_loop(0, 2 * steps, one, 0)

    project(1)

    for o in range(2):

        def prims_of(k, carry, o=o):
            first = regroup[o, 0, k].reshape(group_rows, 128).astype(F32)
            second = regroup[o, 1, k].reshape(group_rows, 128).astype(F32)
            third = regroup[o, 2, k].reshape(group_rows, 128).astype(F32)
            prim = jnp.where(low_half, first, swap_halves(second))
            prim_last = jnp.where(low_half, third, 0.0)
            at = pl.multiple_of(k * 256, 256)
            proj_lhs[0, o, :, pl.ds(at, 128)] = prim.astype(LOW)
            proj_lhs[0, o, :, pl.ds(at + 128, 128)] = prim_last.astype(LOW)
            prim_t[o, k, 0:128, :] = prim.T.astype(LOW)
            prim_t[o, k, 128:192, :] = prim_last.T[0:64].astype(LOW)
            return carry

        lax.fori_loop(0, side, prims_of, 0)

    skip = 2 * half - width

    def collect(kind, o, j, skipped):
        total = part_in[kind, o, j, 0, :, skipped:].astype(F32)
        for k in range(1, side):
            total = total + part_in[kind, o, j, k, :, skipped:].astype(F32)
        return total

    def t_copy():
        return pltpu.make_async_remote_copy(
            src_ref=prim_t.at[1 - c],
            dst_ref=prim_in,
            send_sem=t_send,
            recv_sem=t_recv,
            device_id=twin(),
            device_id_type=MESH,
        )

    t_copy().start()
    own_squares = jnp.zeros((1, 128), F32)
    for n in range(2 * steps):
        o, j = n % 2, n // 2
        for i in range(1, side):
            r_arrival(1, o, j, (place(1 - o) + i) % side).wait_recv()
        skipped = skip if (o, j) == (1, 0) else 0
        columns = collect(1, o, j, skipped)
        at = o * offset + j * wide + skipped
        tan_sum[:, at : at + columns.shape[1]] = columns
        column_squares = jnp.sum(columns * columns, axis=0, keepdims=True)
        for lane in range(0, columns.shape[1], 128):
            own_squares = own_squares + column_squares[:, lane : lane + 128]
    squares[me] = jnp.broadcast_to(jnp.sum(own_squares, axis=1, keepdims=True), (8, 128))

    def q_copy(t):
        return pltpu.make_async_remote_copy(
            src_ref=squares.at[me],
            dst_ref=squares.at[me],
            send_sem=q_send.at[t],
            recv_sem=q_recv.at[me],
            device_id={"tensor": t},
            device_id_type=MESH,
        )

    def q_start(i, carry):
        q_copy((me + i) % n_t).start()
        return carry

    lax.fori_loop(1, n_t, q_start, 0)
    def q_wait(i, carry):
        t = (me + i) % n_t
        pltpu.make_async_remote_copy(
            src_ref=squares.at[t],
            dst_ref=squares.at[t],
            send_sem=q_send.at[t],
            recv_sem=q_recv.at[t],
            device_id={"tensor": t},
            device_id_type=MESH,
        ).wait_recv()
        return carry

    lax.fori_loop(1, n_t, q_wait, 0)
    square_sum = jnp.sum(squares[...], axis=0)[0:1, 0:1]
    divisor = jnp.sqrt(square_sum / (img * width)) + 0.1
    normal = (tan_sum[...] / divisor).astype(LOW)
    tangent_out[...] = normal
    cot_copy.wait()
    up_rows = (cot_local[...].astype(F32) - normal.astype(F32)).astype(LOW)

    starts = (0, 384, 640, 1024)
    sizes = (384, 256, 384, 256)

    def of(pair, p):
        return pair[p % 2].at[p // 2]

    for p in range(4):
        for o in range(2):
            at = o * offset + starts[p]
            of(upstream, p)[o] = up_rows[:, at : at + sizes[p]]

    def u_copy(o, p, k):
        return pltpu.make_async_remote_copy(
            src_ref=of(upstream, p).at[o],
            dst_ref=of(up_all, p).at[c, pl.ds(place(1 - o) * rows, rows)],
            send_sem=u_send.at[o, p, k],
            recv_sem=u_recv.at[c, p, place(1 - o)],
            device_id={"tensor": line(1 - o, k), "dp": z * 2 + o},
            device_id_type=MESH,
        )

    def u_arrival(core, p, k):
        return pltpu.make_async_remote_copy(
            src_ref=of(upstream, p).at[c],
            dst_ref=of(up_all, p).at[core, pl.ds(k * rows, rows)],
            send_sem=u_send.at[c, p, k],
            recv_sem=u_recv.at[core, p, k],
            device_id={"tensor": line(1 - c, k), "dp": z * 2 + core},
            device_id_type=MESH,
        )

    def up_targets(step):
        for i in range(1, side + 1):
            other = 1 - c
            step(other, (place(1 - other) + i) % side)
            if i < side:
                step(c, (place(1 - c) + i) % side)

    def up_leaves(p):
        def step(o, k):
            if p > 1:
                u_copy(o, p - 2, k).wait_send()
            u_copy(o, p, k).start()

        up_targets(step)

    up_leaves(0)
    for p in range(4):
        of(up_all, p)[c, pl.ds(place(1 - c) * rows, rows), :] = of(upstream, p)[c]
    up_leaves(1)

    own = place(c)

    def g_copy(p, k):
        return pltpu.make_async_remote_copy(
            src_ref=of(grad_send, p).at[k],
            dst_ref=of(grad_in, p).at[place(c)],
            send_sem=g_send.at[p, k],
            recv_sem=g_recv.at[p, place(c)],
            device_id={"tensor": line(c, k)},
            device_id_type=MESH,
        )

    def g_arrival(p, k):
        return pltpu.make_async_remote_copy(
            src_ref=of(grad_in, p).at[k],
            dst_ref=of(grad_in, p).at[k],
            send_sem=g_send.at[p, k],
            recv_sem=g_recv.at[p, k],
            device_id={"tensor": line(c, k)},
            device_id_type=MESH,
        )

    def product(left, core, p):
        return jnp.dot(
            left.reshape(side * 192, group_rows),
            of(up_all, p)[core],
            preferred_element_type=F32,
        )

    def line_part(p):
        for i in range(1, side):
            u_arrival(c, p, (place(1 - c) + i) % side).wait_recv()
        for k in range(side):
            u_arrival(1 - c, p, k).wait_recv()
        if p + 2 < 4:
            up_leaves(p + 2)
        both_cores = product(prim_t[c], c, p) + product(prim_in[...], 1 - c, p)
        of(grad_send, p)[...] = both_cores.astype(LOW).reshape(side, 192, sizes[p])
        for i in range(1, side):
            k = (own + i) % side
            if p > 1:
                g_copy(p - 2, k).wait_send()
            g_copy(p, k).start()
        of(grad_in, p)[own] = of(grad_send, p)[own]

    def owned(k):
        return pl.ds(pl.multiple_of((k // 2) * chunk_rows, 16), chunk_rows)

    def z_copy(p, k, source):
        return pltpu.make_async_remote_copy(
            src_ref=of(z_out, p).at[owned(k)],
            dst_ref=z_in[p % 2].at[source],
            send_sem=z_send.at[p, k],
            recv_sem=z_recv.at[p % 2, source],
            device_id={"dp": k * 2 + c},
            device_id_type=MESH,
        )

    def c_place(way, hop):
        return (z - (1 - 2 * way) * (1 - 2 * c) * hop + n_z) % n_z

    def c_copy(way, hop, piece):
        at = c_place(way, hop)
        return pltpu.make_async_remote_copy(
            src_ref=final[piece].at[c, at % 2, owned(at)],
            dst_ref=final[piece].at[c, at % 2, owned(at)],
            send_sem=c_send.at[way, hop % (n_z // 2), piece],
            recv_sem=c_recv.at[at, piece],
            device_id={"dp": c_place(way, -1) * 2 + c},
            device_id_type=MESH,
        )

    def s_copy(which, at, piece):
        return pltpu.make_async_remote_copy(
            src_ref=final[piece].at[which, at % 2, owned(at)],
            dst_ref=final[piece].at[which, at % 2, owned(at)],
            send_sem=s_send.at[at, piece],
            recv_sem=s_recv.at[at, piece],
            device_id=twin(),
            device_id_type=MESH,
        )

    def z_loop(step):
        def one(i, carry):
            step((z + i) % n_z)
            return carry

        lax.fori_loop(1, n_z, one, 0)

    def z_part(p, step):
        def one(i, inner):
            k = (z + i) % n_z

            @pl.when(k % 2 == p // 2)
            def _():
                step(k)

            return inner

        lax.fori_loop(1, n_z, one, 0)

    def to_owners(p):
        for i in range(1, side):
            g_arrival(p, (own + i) % side).wait_recv()
        total = of(grad_in, p)[0].astype(F32)
        for k in range(1, side):
            total = total + of(grad_in, p)[k].astype(F32)
        of(z_out, p)[...] = total.astype(LOW)
        z_part(p, lambda k: z_copy(p, k, z).start())

    t_copy().wait_recv()
    line_part(0)
    line_part(1)
    to_owners(0)
    line_part(2)
    to_owners(1)
    line_part(3)
    to_owners(2)
    to_owners(3)

    project(0)

    for piece in range(2):
        z_in[piece][z] = z_out[piece][z % 2, owned(z), :]
        z_loop(lambda k, piece=piece: z_copy(piece, k, k).wait_recv())
        total = z_in[piece][0].astype(F32)
        for k in range(1, n_z):
            total = total + z_in[piece][k].astype(F32)
        final[piece][c, z % 2, owned(z), :] = (total * (1.0 / (2 * n_z))).astype(LOW)
        c_copy(0, 0, piece).start()
        c_copy(1, 0, piece).start()
        s_copy(c, z, piece).start()
    for hop in range(1, reach[0] + 1):
        if hop == reach[0]:
            gathered(0)
            for o in range(2):
                for j in range(steps):
                    skipped = skip if (o, j) == (1, 0) else 0
                    at = o * offset + j * wide + skipped
                    image_out[:, at : at + wide - skipped] = collect(0, o, j, skipped).astype(LOW)
        for piece in range(2):
            for way in range(2):
                if hop <= reach[way]:
                    c_copy(way, hop, piece).wait_recv()
                    if hop < reach[way]:
                        c_copy(way, hop, piece).start()
                    s_copy(c, c_place(way, hop), piece).start()

    ring(lambda t: in_copy(1, t).wait_send())
    ring(lambda t: in_copy(2, t).wait_send())
    x_sent()
    for i in range(1, side):
        w_copy((place(c) + i) % side).wait_send()
        for o in range(2):
            for s in range(slots):
                for q in range(side if o == 0 else 1):
                    p_copy(s, o, (place(o) + i) % side, q).wait_send()
        for p in (2, 3):
            g_copy(p, (place(c) + i) % side).wait_send()

    def r_sent(n, carry):
        o = n % 2
        for kind in range(2):
            for i in range(1, side):
                r_copy(kind, o, n // 2, (place(1 - o) + i) % side).wait_send()
        return carry

    lax.fori_loop(0, 2 * steps, r_sent, 0)
    for k in range(side):
        f_copy(k).wait_send()

    t_copy().wait_send()
    for p in (2, 3):
        up_targets(lambda o, k, p=p: u_copy(o, p, k).wait_send())

    def q_sent(i, carry):
        q_copy((me + i) % n_t).wait_send()
        return carry

    lax.fori_loop(1, n_t, q_sent, 0)
    for p in range(4):
        z_part(p, lambda k, p=p: z_copy(p, k, z).wait_send())
    for way in range(2):
        for hop in range(reach[way]):
            for piece in range(2):
                c_copy(way, hop, piece).wait_send()
    for at in range(n_z):
        for piece in range(2):
            s_copy(c, at, piece).wait_send()
            s_copy(1 - c, at, piece).wait_recv()
    for which in range(2):
        for p in range(4):
            grad_out[which, :, starts[p] : starts[p] + sizes[p]] = final[p % 2][which, p // 2]


def on_device(n_t, n_dp, qkv_img, tan_img, txt_kv, head_table, out_weight, cotangent):
    rows, width = qkv_img.shape[1], qkv_img.shape[3]
    slots = head_table.shape[1]
    side = 4
    n_z = n_dp // 2
    txt_len = txt_kv.shape[2]
    img = n_t * rows
    keys = img + txt_len
    keys_pad = -(-keys // 128) * 128
    half = -(-width // 256) * 128
    offset = width - half
    dims = (n_t, side, n_z, slots, rows, keys, keys_pad, half, offset, width, txt_len)
    dma = pltpu.SemaphoreType.DMA
    vmem = pl.BlockSpec(memory_space=pltpu.VMEM)
    hbm = pl.BlockSpec(memory_space=pl.ANY)

    def both(*shape):
        return [pltpu.VMEM(shape + (384,), LOW), pltpu.VMEM(shape + (256,), LOW)]

    image, tangent, grad = pl.pallas_call(
        functools.partial(body, dims),
        out_shape=(
            jax.ShapeDtypeStruct((rows, width), LOW),
            jax.ShapeDtypeStruct((rows, width), LOW),
            jax.ShapeDtypeStruct((2, 192, half), LOW),
        ),
        in_specs=[pl.BlockSpec(memory_space=pltpu.SMEM)] + [hbm] * 5,
        out_specs=(vmem, vmem, vmem),
        scratch_shapes=[
            pltpu.VMEM((rows, width), LOW),
            pltpu.VMEM((3, rows, width), LOW),
            pltpu.VMEM((3, rows, width), LOW),
            pltpu.VMEM((slots, txt_len, 256), LOW),
            pltpu.VMEM((6, width // 128, rows, 128), LOW),
            pltpu.VMEM((slots, n_t, rows, 384), LOW),
            pltpu.VMEM((slots, n_t, rows, 384), LOW),
            pltpu.VMEM((384, 256), LOW),
            pltpu.VMEM((slots, 128, 2 * keys_pad), LOW),
            pltpu.VMEM((slots, 2 * keys_pad, 128), LOW),
            pltpu.VMEM((slots, side, side, rows, 128), LOW),
            pltpu.VMEM((2, slots, side, side, rows, 128), LOW),
            pltpu.VMEM((2, side * 256, half), LOW),
            pltpu.VMEM((2, 2, side * rows, side * 256), LOW),
            pltpu.VMEM((2, side, 192, side * rows), LOW),
            pltpu.VMEM((2, 2, 2, side, rows, half // 2), LOW),
            pltpu.VMEM((2, 2, 2, side, rows, half // 2), LOW),
            pltpu.VMEM((rows, width), F32),
            pltpu.VMEM((n_t, 8, 128), F32),
            *both(2, 2, rows),
            *both(2, 2, side * rows),
            pltpu.VMEM((side, 192, side * rows), LOW),
            *both(2, side, 192),
            *both(2, side, 192),
            *both(2, 192),
            *both(n_z, 2 * 192 // n_z),
            *both(2, 2, 192),
            dma((slots, n_t)),
            dma((slots, n_t)),
            dma((side,)),
            dma((side,)),
            dma((side, 2, n_z // 2)),
            dma((side, n_z)),
            dma((side,)),
            dma((side,)),
            dma((9 + slots,)),
            dma((2, slots, side, side)),
            dma((2, slots, side, side)),
            dma((2, 2, 2, side)),
            dma((2, 2, 2, side)),
            dma((n_t,)),
            dma((n_t,)),
            dma((2, 4, side)),
            dma((2, 4, side)),
            dma,
            dma,
            dma((4, side)),
            dma((4, side)),
            dma((4, n_z)),
            dma((2, n_z)),
            dma((2, n_z // 2, 2)),
            dma((n_z, 2)),
            dma((n_z, 2)),
            dma((n_z, 2)),
        ],
        compiler_params=pltpu.CompilerParams(
            collective_id=0, has_side_effects=True, vmem_limit_bytes=56 * 1024 * 1024
        ),
    )(
        head_table.T,
        jnp.transpose(qkv_img[0], (1, 0, 2)),
        jnp.transpose(tan_img[0], (1, 0, 2)),
        txt_kv[0],
        out_weight,
        cotangent[0],
    )
    return pl.pallas_call(
        finish,
        out_shape=(
            jax.ShapeDtypeStruct((rows, width), LOW),
            jax.ShapeDtypeStruct((rows, width), LOW),
            jax.ShapeDtypeStruct((slots * 64, width), F32),
        ),
        in_specs=[hbm, hbm, hbm],
        out_specs=(hbm, hbm, hbm),
        scratch_shapes=[
            pltpu.VMEM((2, rows, width), LOW),
            pltpu.VMEM((2, 192, half), LOW),
            pltpu.VMEM((192, width), F32),
            dma((4,)),
            dma((4,)),
            dma((4,)),
        ],
    )(image, tangent, grad)


def solution(mesh):
    n_t, n_dp = mesh.shape["tensor"], mesh.shape["dp"]

    def step(*args):
        image_out, tangent_out, weight_grad = on_device(n_t, n_dp, *args)
        return image_out[None], tangent_out[None], weight_grad

    return jax.shard_map(
        step,
        mesh=mesh,
        in_specs=(
            P("dp", "tensor", None, None),
            P("dp", "tensor", None, None),
            P("dp", "tensor", None, None),
            P(),
            P("tensor", None),
            P("dp", "tensor", None),
        ),
        out_specs=(P("dp", "tensor", None), P("dp", "tensor", None), P("tensor", None)),
        check_vma=False,
    )
```

```python
import functools

import jax
import jax.numpy as jnp
from jax import lax
from jax.experimental import pallas as pl
from jax.experimental.pallas import tpu as pltpu
from jax.sharding import PartitionSpec as P

MESH = pl.DeviceIdType.MESH
F32 = jnp.float32
LOW = jnp.bfloat16


def swap_halves(value):
    return pltpu.roll(value, 64, 1)


def finish(
    image, tangent, grad, image_out, tangent_out, grad_out, pair, held, wide, in_sem, out_sem, way_sem
):
    half = grad.shape[2]
    width = image.shape[1]
    skip = 2 * half - width
    blocks = 4
    tall = grad.shape[1] // blocks

    def load(i):
        rows = pl.ds(i * tall, tall)
        return pltpu.make_async_copy(grad.at[:, rows], held.at[:, rows], in_sem.at[i])

    def store(i):
        rows = pl.ds(i * tall, tall)
        return pltpu.make_async_copy(wide.at[rows], grad_out.at[rows], out_sem.at[i])

    for i in range(blocks):
        load(i).start()
    there = (
        pltpu.make_async_copy(image, pair.at[0], way_sem.at[0]),
        pltpu.make_async_copy(tangent, pair.at[1], way_sem.at[1]),
    )
    back = (
        pltpu.make_async_copy(pair.at[0], image_out, way_sem.at[2]),
        pltpu.make_async_copy(pair.at[1], tangent_out, way_sem.at[3]),
    )
    for copy in there:
        copy.start()
    for i in range(blocks):
        load(i).wait()
        rows = pl.ds(i * tall, tall)
        wide[rows, 0:half] = held[0, rows].astype(F32)
        wide[rows, half:width] = held[1, rows, skip:].astype(F32)
        store(i).start()
    for copy, after in zip(there, back):
        copy.wait()
        after.start()
    for i in range(blocks):
        store(i).wait()
    for copy in back:
        copy.wait()


def body(
    dims,
    table,
    qkv,
    tan,
    txt,
    weight,
    cot,
    image_out,
    tangent_out,
    grad_out,
    cot_local,
    qkv_local,
    tan_local,
    txt_local,
    staged,
    outbox,
    arrived,
    text_pad,
    score_rhs,
    value_rhs,
    attn,
    regroup,
    group_weight,
    proj_lhs,
    prim_t,
    part_out,
    part_in,
    tan_sum,
    squares,
    upstream_a,
    upstream_b,
    up_all_a,
    up_all_b,
    prim_in,
    grad_send_a,
    grad_send_b,
    grad_in_a,
    grad_in_b,
    z_out_a,
    z_out_b,
    z_in_a,
    z_in_b,
    final_a,
    final_b,
    a_send,
    a_recv,
    w_send,
    w_recv,
    x_send,
    x_recv,
    f_send,
    f_recv,
    own_sem,
    p_send,
    p_recv,
    r_send,
    r_recv,
    q_send,
    q_recv,
    u_send,
    u_recv,
    t_send,
    t_recv,
    g_send,
    g_recv,
    z_send,
    z_recv,
    c_send,
    c_recv,
    s_send,
    s_recv,
):
    n_t, side, n_z, slots, rows, keys, keys_pad, half, offset, width, txt_len = dims
    me = lax.axis_index("tensor")
    dp = lax.axis_index("dp")
    x = me // side
    y = me % side
    z = dp // 2
    c = dp % 2
    upstream = (upstream_a, upstream_b)
    up_all = (up_all_a, up_all_b)
    grad_send = (grad_send_a, grad_send_b)
    grad_in = (grad_in_a, grad_in_b)
    z_out = (z_out_a, z_out_b)
    z_in = (z_in_a, z_in_b)
    final = (final_a, final_b)
    img = n_t * rows
    group_rows = side * rows

    def line(o, k):
        return (1 - o) * (x * side + k) + o * (k * side + y)

    def place(o):
        return (1 - o) * y + o * x

    def twin():
        return {"dp": z * 2 + (1 - c)}

    low_half = lax.broadcasted_iota(jnp.int32, (1, 128), 1) < 64

    cot_copy = pltpu.make_async_copy(cot, cot_local, own_sem.at[1 + slots])
    txt_copy = pltpu.make_async_copy(txt, txt_local, own_sem.at[2 + slots])
    loads = [
        pltpu.make_async_copy(whole.at[kind], local.at[kind], own_sem.at[3 + slots + 3 * n + kind])
        for n, (whole, local) in enumerate(((qkv, qkv_local), (tan, tan_local)))
        for kind in range(3)
    ]
    for copy in loads:
        copy.start()
    txt_copy.start()
    cot_copy.start()

    barrier = pltpu.get_barrier_semaphore()

    def greet(i, carry):
        t = ((x + i // side) % side) * side + (y + i % side) % side
        pl.semaphore_signal(barrier, inc=1, device_id={"tensor": t}, device_id_type=MESH)
        return carry

    lax.fori_loop(1, n_t, greet, 0)

    def greet_z(i, carry):
        pl.semaphore_signal(
            barrier, inc=1, device_id={"dp": ((z + i) % n_z) * 2 + c}, device_id_type=MESH
        )
        return carry

    lax.fori_loop(1, n_z, greet_z, 0)
    pl.semaphore_signal(barrier, inc=1, device_id=twin(), device_id_type=MESH)
    for o in range(2):
        for i in range(1, side):
            pl.semaphore_signal(
                barrier,
                inc=1,
                device_id={"tensor": line(o, (place(o) + i) % side), "dp": z * 2 + (1 - c)},
                device_id_type=MESH,
            )

    for o in range(2):
        for k in range(side):
            group_weight[o, k * 256 + 192 : k * 256 + 256, :] = jnp.zeros((64, half), LOW)

    def text_rows(s):
        text_pad[320:384, :] = jnp.zeros((64, 256), LOW)
        text_pad[0:txt_len, :] = txt_local[s]
        kv = text_pad[:, 0:128].astype(F32)
        dkv = text_pad[:, 128:256].astype(F32)
        key_pair = jnp.where(low_half, kv, swap_halves(dkv))
        val_pair = jnp.where(low_half, swap_halves(kv), dkv)
        key_t = key_pair.T.astype(LOW)
        score_rhs[s, 0:64, 0:keys_pad] = jnp.zeros((64, keys_pad), LOW)
        score_rhs[s, 64:128, img:keys_pad] = key_t[0:64]
        score_rhs[s, :, keys_pad + img : 2 * keys_pad] = key_t
        value_rhs[s, img:keys_pad, :] = val_pair.astype(LOW)
        value_rhs[s, keys_pad + img : 2 * keys_pad, :] = jnp.where(low_half, 0.0, kv).astype(LOW)

    for n, local in enumerate((qkv_local, tan_local)):
        for kind in range(3):
            loads[3 * n + kind].wait()
            for page in range(width // 128):
                staged[3 * n + kind, page] = local[kind, :, page * 128 : page * 128 + 128]

    def pick(s, t):
        head = jnp.maximum(table[s, t], 0)
        page = lax.shift_right_logical(head, 1)
        odd = jnp.full((1, 128), lax.bitwise_and(head, 1), jnp.int32) == 1

        def pair(first, second):
            a = staged[first, page]
            b = staged[second, page]
            return jnp.where(
                low_half, jnp.where(odd, swap_halves(a), a), jnp.where(odd, b, swap_halves(b))
            )

        outbox[s, t, :, 0:128] = pair(3, 0) * jnp.asarray(0.125, LOW)
        outbox[s, t, :, 128:256] = pair(1, 4)
        outbox[s, t, :, 256:384] = pair(2, 5)

    pl.semaphore_wait(barrier, n_t + n_z - 1 + 2 * (side - 1))

    def in_copy(s, t):
        return pltpu.make_async_remote_copy(
            src_ref=outbox.at[s, t],
            dst_ref=arrived.at[s, me],
            send_sem=a_send.at[s, t],
            recv_sem=a_recv.at[s, me],
            device_id={"tensor": t},
            device_id_type=MESH,
        )

    def ring(step, first=1, last=n_t):
        def one(i, carry):
            step(((x + i // side) % side) * side + (y + i % side) % side)
            return carry

        lax.fori_loop(first, last, one, 0)

    def in_own(s):
        return pltpu.make_async_copy(outbox.at[s, me], arrived.at[s, me], own_sem.at[1 + s])

    half_at = pl.multiple_of(c * offset, 128)

    chunk_rows = 2 * 192 // n_z
    chunk_cols = half // 2

    def w_span(k, at):
        return (
            pl.ds(pl.multiple_of(k * 256 + (at // 2) * chunk_rows, 16), chunk_rows),
            pl.ds(pl.multiple_of((at % 2) * chunk_cols, 128), chunk_cols),
        )

    def w_copy(k):
        return pltpu.make_async_remote_copy(
            src_ref=weight.at[
                pl.ds(pl.multiple_of((z // 2) * chunk_rows, 16), chunk_rows),
                pl.ds(pl.multiple_of(c * offset + (z % 2) * chunk_cols, 128), chunk_cols),
            ],
            dst_ref=group_weight.at[(c,) + w_span(place(c), z)],
            send_sem=w_send.at[k],
            recv_sem=w_recv.at[place(c)],
            device_id={"tensor": line(c, k)},
            device_id_type=MESH,
        )

    def w_arrival(k):
        return pltpu.make_async_remote_copy(
            src_ref=group_weight.at[(c,) + w_span(k, z)],
            dst_ref=group_weight.at[(c,) + w_span(k, z)],
            send_sem=w_send.at[k],
            recv_sem=w_recv.at[k],
            device_id={"tensor": line(c, k)},
            device_id_type=MESH,
        )

    def x_copy(k, at, way, hop):
        return pltpu.make_async_remote_copy(
            src_ref=group_weight.at[(c,) + w_span(k, at)],
            dst_ref=group_weight.at[(c,) + w_span(k, at)],
            send_sem=x_send.at[k, way, hop],
            recv_sem=x_recv.at[k, at],
            device_id={"dp": ((z + 1 - 2 * way + n_z) % n_z) * 2 + c},
            device_id_type=MESH,
        )

    reach = (n_z // 2, n_z // 2 - 1)

    def x_step(hop):
        for way in range(2):
            if hop >= 1 and hop <= reach[way]:
                at = (z + (2 * way - 1) * hop + n_z) % n_z
                for i in range(1, side):
                    k = (place(c) + i) % side
                    x_copy(k, at, way, hop % side).wait_recv()
                    if hop < reach[way]:
                        x_copy(k, at, way, hop).start()
            if hop == 0:
                for i in range(1, side):
                    x_copy((place(c) + i) % side, z, way, 0).start()

    def x_sent():
        for way in range(2):
            for hop in range(reach[way]):
                at = (z + (2 * way - 1) * hop + n_z) % n_z
                for i in range(1, side):
                    x_copy((place(c) + i) % side, at, way, hop).wait_send()

    def w_own():
        return pltpu.make_async_copy(
            weight.at[:, pl.ds(half_at, half)],
            group_weight.at[c, pl.ds(place(c) * 256, 192)],
            own_sem.at[0],
        )

    def f_copy(k):
        return pltpu.make_async_remote_copy(
            src_ref=group_weight.at[c, pl.ds(k * 256, 192)],
            dst_ref=group_weight.at[c, pl.ds(k * 256, 192)],
            send_sem=f_send.at[k],
            recv_sem=f_recv.at[k],
            device_id=twin(),
            device_id_type=MESH,
        )

    def f_arrival(k):
        return pltpu.make_async_remote_copy(
            src_ref=group_weight.at[1 - c, pl.ds(k * 256, 192)],
            dst_ref=group_weight.at[1 - c, pl.ds(k * 256, 192)],
            send_sem=f_send.at[k],
            recv_sem=f_recv.at[k],
            device_id=twin(),
            device_id_type=MESH,
        )

    w_own().start()
    for i in range(1, side):
        w_copy((place(c) + i) % side).start()

    def depart(s):
        def one(t):
            pick(s, t)
            in_copy(s, t).start()

        ring(one)

    early = 6

    def first_slot(t):
        pick(0, t)
        in_copy(0, t).start()

    ring(first_slot, 1, early)
    ring(lambda t: pick(0, t), early, n_t)
    for i in range(1, side):
        w_arrival((place(c) + i) % side).wait_recv()
    x_step(0)
    ring(lambda t: in_copy(0, t).start(), early, n_t)
    depart(1)
    txt_copy.wait()
    for s in range(slots):
        pick(s, me)
        in_own(s).start()
        text_rows(s)
    x_step(1)
    ring(lambda t: pick(2, t))
    x_step(2)

    def last_slot(t):
        in_copy(0, t).wait_send()
        in_copy(2, t).start()

    ring(last_slot)

    def p_copy(s, o, k, q):
        if o == 0:
            source, target = attn.at[s, q, k], regroup.at[0, s, y, q]
        else:
            source, target = attn.at[s, k], regroup.at[1, s, x]
        return pltpu.make_async_remote_copy(
            src_ref=source,
            dst_ref=target,
            send_sem=p_send.at[o, s, k, q],
            recv_sem=p_recv.at[o, s, place(o), q],
            device_id={"tensor": line(o, k)},
            device_id_type=MESH,
        )

    def p_arrival(s, o, k, q):
        target = regroup.at[0, s, k, q] if o == 0 else regroup.at[1, s, k]
        return pltpu.make_async_remote_copy(
            src_ref=target,
            dst_ref=target,
            send_sem=p_send.at[o, s, k, q],
            recv_sem=p_recv.at[o, s, k, q],
            device_id={"tensor": line(o, k)},
            device_id_type=MESH,
        )

    def one_slot(s, carry):
        def arrival(i, inner):
            t = (me + i) % n_t
            pltpu.make_async_remote_copy(
                src_ref=outbox.at[s, t],
                dst_ref=arrived.at[s, t],
                send_sem=a_send.at[s, t],
                recv_sem=a_recv.at[s, t],
                device_id={"tensor": t},
                device_id_type=MESH,
            ).wait_recv()
            return inner

        lax.fori_loop(1, n_t, arrival, 0)
        in_own(s).wait()
        key_t = arrived[s, :, :, 128:256].reshape(img, 128).astype(F32).T.astype(LOW)
        score_rhs[s, 64:128, 0:img] = key_t[0:64]
        score_rhs[s, :, keys_pad : keys_pad + img] = key_t
        val_pair = arrived[s, :, :, 256:384].reshape(img, 128)
        value_rhs[s, 0:img, :] = val_pair
        value_rhs[s, keys_pad : keys_pad + img, :] = jnp.where(
            low_half, 0.0, swap_halves(val_pair.astype(F32))
        ).astype(LOW)
        filled = jnp.where(jnp.full((1, 128), table[s, me], jnp.int32) >= 0, 1.0, 0.0)

        def one_block(turn, inner):
            q = (x + 1 + turn) % side
            lhs = arrived[s, pl.ds(q * side, side), :, 0:128].reshape(group_rows, 128)
            scores = jnp.dot(lhs, score_rhs[s, :, 0:keys_pad], preferred_element_type=F32)
            tangents = jnp.dot(
                lhs, score_rhs[s, :, keys_pad : 2 * keys_pad], preferred_element_type=F32
            )
            valid = lax.broadcasted_iota(jnp.int32, (1, 128), 1) < keys - (keys_pad - 128)
            scores = jnp.concatenate(
                [
                    scores[:, : keys_pad - 128],
                    jnp.where(valid, scores[:, keys_pad - 128 :], -1e30),
                ],
                1,
            )
            top = jnp.max(scores, axis=1, keepdims=True)
            raised = jnp.exp(scores - top)
            total = jnp.sum(raised, axis=1, keepdims=True)
            mean = jnp.sum(raised * tangents, axis=1, keepdims=True) / total
            shifted = raised * (tangents - mean)
            joined = jnp.dot(
                raised.astype(LOW), value_rhs[s, 0:keys_pad, :], preferred_element_type=F32
            ) + jnp.dot(
                shifted.astype(LOW),
                value_rhs[s, keys_pad : 2 * keys_pad, :],
                preferred_element_type=F32,
            )
            joined = (joined / total * filled).astype(LOW)
            attn[s, q] = joined.reshape(side, rows, 128)
            for i in range(1, side):
                p_copy(s, 0, (y + i) % side, q).start()

            @pl.when(turn < side - 1)
            def _():
                p_copy(s, 1, q, 0).start()

            return inner

        lax.fori_loop(0, side, one_block, 0)
        regroup[0, s, y] = attn[s, :, y]
        regroup[1, s, x] = attn[s, x]

        @pl.when(s == 0)
        def _():
            x_step(3)

        @pl.when(s == 1)
        def _():
            x_step(4)
            w_own().wait()
            for k in range(side):
                f_copy(k).start()


        return carry

    lax.fori_loop(0, slots, one_slot, 0)

    steps = 2
    wide = half // steps

    def r_copy(kind, o, j, k):
        return pltpu.make_async_remote_copy(
            src_ref=part_out.at[kind, o, j, k],
            dst_ref=part_in.at[kind, o, j, place(1 - o)],
            send_sem=r_send.at[kind, o, j, k],
            recv_sem=r_recv.at[kind, o, j, place(1 - o)],
            device_id={"tensor": line(1 - o, k)},
            device_id_type=MESH,
        )

    def r_arrival(kind, o, j, k):
        return pltpu.make_async_remote_copy(
            src_ref=part_out.at[kind, o, j, k],
            dst_ref=part_in.at[kind, o, j, k],
            send_sem=r_send.at[kind, o, j, k],
            recv_sem=r_recv.at[kind, o, j, k],
            device_id={"tensor": line(1 - o, k)},
            device_id_type=MESH,
        )

    for o in range(2):
        for s in range(slots):
            for i in range(1, side):
                k = (place(o) + i) % side
                for q in range(side if o == 0 else 1):
                    p_arrival(s, o, k, q).wait_recv()

        def tangents_of(k, carry, o=o):
            first = regroup[o, 0, k].reshape(group_rows, 128).astype(F32)
            second = regroup[o, 1, k].reshape(group_rows, 128).astype(F32)
            third = regroup[o, 2, k].reshape(group_rows, 128).astype(F32)
            tang = jnp.where(low_half, swap_halves(first), second)
            tang_last = jnp.where(low_half, swap_halves(third), 0.0)
            at = pl.multiple_of(k * 256, 256)
            proj_lhs[1, o, :, pl.ds(at, 128)] = tang.astype(LOW)
            proj_lhs[1, o, :, pl.ds(at + 128, 128)] = tang_last.astype(LOW)
            return carry

        lax.fori_loop(0, side, tangents_of, 0)

    for k in range(side):
        f_arrival(k).wait_recv()

    def project(kind):
        def one(n, carry):
            o = n % 2
            j = n // 2
            span = pl.ds(pl.multiple_of(j * wide, 128), wide)
            part = jnp.dot(
                proj_lhs[kind, o], group_weight[o, :, span], preferred_element_type=F32
            ).astype(LOW)
            for k in range(side):
                part_out[kind, o, j, k] = part[k * rows : (k + 1) * rows]
            own = place(1 - o)
            for i in range(1, side):
                r_copy(kind, o, j, (own + i) % side).start()
            part_in[kind, o, j, own] = part_out[kind, o, j, own]
            return carry

        lax.fori_loop(0, 2 * steps, one, 0)

    def gathered(kind):
        def one(n, carry):
            for i in range(1, side):
                r_arrival(kind, n % 2, n // 2, (place(1 - n % 2) + i) % side).wait_recv()
            return carry

        lax.fori_loop(0, 2 * steps, one, 0)

    project(1)

    for o in range(2):

        def prims_of(k, carry, o=o):
            first = regroup[o, 0, k].reshape(group_rows, 128).astype(F32)
            second = regroup[o, 1, k].reshape(group_rows, 128).astype(F32)
            third = regroup[o, 2, k].reshape(group_rows, 128).astype(F32)
            prim = jnp.where(low_half, first, swap_halves(second))
            prim_last = jnp.where(low_half, third, 0.0)
            at = pl.multiple_of(k * 256, 256)
            proj_lhs[0, o, :, pl.ds(at, 128)] = prim.astype(LOW)
            proj_lhs[0, o, :, pl.ds(at + 128, 128)] = prim_last.astype(LOW)
            prim_t[o, k, 0:128, :] = prim.T.astype(LOW)
            prim_t[o, k, 128:192, :] = prim_last.T[0:64].astype(LOW)
            return carry

        lax.fori_loop(0, side, prims_of, 0)

    skip = 2 * half - width

    def collect(kind, o, j, skipped):
        total = part_in[kind, o, j, 0, :, skipped:].astype(F32)
        for k in range(1, side):
            total = total + part_in[kind, o, j, k, :, skipped:].astype(F32)
        return total

    def t_copy():
        return pltpu.make_async_remote_copy(
            src_ref=prim_t.at[1 - c],
            dst_ref=prim_in,
            send_sem=t_send,
            recv_sem=t_recv,
            device_id=twin(),
            device_id_type=MESH,
        )

    t_copy().start()
    own_squares = jnp.zeros((1, 128), F32)
    for n in range(2 * steps):
        o, j = n % 2, n // 2
        for i in range(1, side):
            r_arrival(1, o, j, (place(1 - o) + i) % side).wait_recv()
        skipped = skip if (o, j) == (1, 0) else 0
        columns = collect(1, o, j, skipped)
        at = o * offset + j * wide + skipped
        tan_sum[:, at : at + columns.shape[1]] = columns
        column_squares = jnp.sum(columns * columns, axis=0, keepdims=True)
        for lane in range(0, columns.shape[1], 128):
            own_squares = own_squares + column_squares[:, lane : lane + 128]
    squares[me] = jnp.broadcast_to(jnp.sum(own_squares, axis=1, keepdims=True), (8, 128))

    def q_copy(t):
        return pltpu.make_async_remote_copy(
            src_ref=squares.at[me],
            dst_ref=squares.at[me],
            send_sem=q_send.at[t],
            recv_sem=q_recv.at[me],
            device_id={"tensor": t},
            device_id_type=MESH,
        )

    def q_start(i, carry):
        q_copy((me + i) % n_t).start()
        return carry

    lax.fori_loop(1, n_t, q_start, 0)
    def q_wait(i, carry):
        t = (me + i) % n_t
        pltpu.make_async_remote_copy(
            src_ref=squares.at[t],
            dst_ref=squares.at[t],
            send_sem=q_send.at[t],
            recv_sem=q_recv.at[t],
            device_id={"tensor": t},
            device_id_type=MESH,
        ).wait_recv()
        return carry

    lax.fori_loop(1, n_t, q_wait, 0)
    square_sum = jnp.sum(squares[...], axis=0)[0:1, 0:1]
    divisor = jnp.sqrt(square_sum / (img * width)) + 0.1
    normal = (tan_sum[...] / divisor).astype(LOW)
    tangent_out[...] = normal
    cot_copy.wait()
    up_rows = (cot_local[...].astype(F32) - normal.astype(F32)).astype(LOW)

    starts = (0, 384, 640, 1024)
    sizes = (384, 256, 384, 256)

    def of(pair, p):
        return pair[p % 2].at[p // 2]

    for p in range(4):
        for o in range(2):
            at = o * offset + starts[p]
            of(upstream, p)[o] = up_rows[:, at : at + sizes[p]]

    def u_copy(o, p, k):
        return pltpu.make_async_remote_copy(
            src_ref=of(upstream, p).at[o],
            dst_ref=of(up_all, p).at[c, pl.ds(place(1 - o) * rows, rows)],
            send_sem=u_send.at[o, p, k],
            recv_sem=u_recv.at[c, p, place(1 - o)],
            device_id={"tensor": line(1 - o, k), "dp": z * 2 + o},
            device_id_type=MESH,
        )

    def u_arrival(core, p, k):
        return pltpu.make_async_remote_copy(
            src_ref=of(upstream, p).at[c],
            dst_ref=of(up_all, p).at[core, pl.ds(k * rows, rows)],
            send_sem=u_send.at[c, p, k],
            recv_sem=u_recv.at[core, p, k],
            device_id={"tensor": line(1 - c, k), "dp": z * 2 + core},
            device_id_type=MESH,
        )

    def up_targets(step):
        for i in range(1, side + 1):
            other = 1 - c
            step(other, (place(1 - other) + i) % side)
            if i < side:
                step(c, (place(1 - c) + i) % side)

    def up_leaves(p):
        def step(o, k):
            if p > 1:
                u_copy(o, p - 2, k).wait_send()
            u_copy(o, p, k).start()

        up_targets(step)

    up_leaves(0)
    for p in range(4):
        of(up_all, p)[c, pl.ds(place(1 - c) * rows, rows), :] = of(upstream, p)[c]
    up_leaves(1)

    own = place(c)

    def g_copy(p, k):
        return pltpu.make_async_remote_copy(
            src_ref=of(grad_send, p).at[k],
            dst_ref=of(grad_in, p).at[place(c)],
            send_sem=g_send.at[p, k],
            recv_sem=g_recv.at[p, place(c)],
            device_id={"tensor": line(c, k)},
            device_id_type=MESH,
        )

    def g_arrival(p, k):
        return pltpu.make_async_remote_copy(
            src_ref=of(grad_in, p).at[k],
            dst_ref=of(grad_in, p).at[k],
            send_sem=g_send.at[p, k],
            recv_sem=g_recv.at[p, k],
            device_id={"tensor": line(c, k)},
            device_id_type=MESH,
        )

    def product(left, core, p):
        return jnp.dot(
            left.reshape(side * 192, group_rows),
            of(up_all, p)[core],
            preferred_element_type=F32,
        )

    def line_part(p):
        for i in range(1, side):
            u_arrival(c, p, (place(1 - c) + i) % side).wait_recv()
        for k in range(side):
            u_arrival(1 - c, p, k).wait_recv()
        if p + 2 < 4:
            up_leaves(p + 2)
        both_cores = product(prim_t[c], c, p) + product(prim_in[...], 1 - c, p)
        of(grad_send, p)[...] = both_cores.astype(LOW).reshape(side, 192, sizes[p])
        for i in range(1, side):
            k = (own + i) % side
            if p > 1:
                g_copy(p - 2, k).wait_send()
            g_copy(p, k).start()
        of(grad_in, p)[own] = of(grad_send, p)[own]

    def owned(k):
        return pl.ds(pl.multiple_of((k // 2) * chunk_rows, 16), chunk_rows)

    def z_copy(p, k, source):
        return pltpu.make_async_remote_copy(
            src_ref=of(z_out, p).at[owned(k)],
            dst_ref=z_in[p % 2].at[source],
            send_sem=z_send.at[p, k],
            recv_sem=z_recv.at[p % 2, source],
            device_id={"dp": k * 2 + c},
            device_id_type=MESH,
        )

    def c_place(way, hop):
        return (z - (1 - 2 * way) * (1 - 2 * c) * hop + n_z) % n_z

    def c_copy(way, hop, piece):
        at = c_place(way, hop)
        return pltpu.make_async_remote_copy(
            src_ref=final[piece].at[c, at % 2, owned(at)],
            dst_ref=final[piece].at[c, at % 2, owned(at)],
            send_sem=c_send.at[way, hop % (n_z // 2), piece],
            recv_sem=c_recv.at[at, piece],
            device_id={"dp": c_place(way, -1) * 2 + c},
            device_id_type=MESH,
        )

    def s_copy(which, at, piece):
        return pltpu.make_async_remote_copy(
            src_ref=final[piece].at[which, at % 2, owned(at)],
            dst_ref=final[piece].at[which, at % 2, owned(at)],
            send_sem=s_send.at[at, piece],
            recv_sem=s_recv.at[at, piece],
            device_id=twin(),
            device_id_type=MESH,
        )

    def z_loop(step):
        def one(i, carry):
            step((z + i) % n_z)
            return carry

        lax.fori_loop(1, n_z, one, 0)

    def z_part(p, step):
        def one(i, inner):
            k = (z + i) % n_z

            @pl.when(k % 2 == p // 2)
            def _():
                step(k)

            return inner

        lax.fori_loop(1, n_z, one, 0)

    def to_owners(p):
        for i in range(1, side):
            g_arrival(p, (own + i) % side).wait_recv()
        total = of(grad_in, p)[0].astype(F32)
        for k in range(1, side):
            total = total + of(grad_in, p)[k].astype(F32)
        of(z_out, p)[...] = total.astype(LOW)
        z_part(p, lambda k: z_copy(p, k, z).start())

    t_copy().wait_recv()
    line_part(0)
    line_part(1)
    to_owners(0)
    line_part(2)
    to_owners(1)
    line_part(3)
    to_owners(2)
    to_owners(3)

    project(0)

    for piece in range(2):
        z_in[piece][z] = z_out[piece][z % 2, owned(z), :]
        z_loop(lambda k, piece=piece: z_copy(piece, k, k).wait_recv())
        total = z_in[piece][0].astype(F32)
        for k in range(1, n_z):
            total = total + z_in[piece][k].astype(F32)
        final[piece][c, z % 2, owned(z), :] = (total * (1.0 / (2 * n_z))).astype(LOW)
        c_copy(0, 0, piece).start()
        c_copy(1, 0, piece).start()
        s_copy(c, z, piece).start()
    for hop in range(1, reach[0] + 1):
        if hop == reach[0]:
            gathered(0)
            for o in range(2):
                for j in range(steps):
                    skipped = skip if (o, j) == (1, 0) else 0
                    at = o * offset + j * wide + skipped
                    image_out[:, at : at + wide - skipped] = collect(0, o, j, skipped).astype(LOW)
        for piece in range(2):
            for way in range(2):
                if hop <= reach[way]:
                    c_copy(way, hop, piece).wait_recv()
                    if hop < reach[way]:
                        c_copy(way, hop, piece).start()
                    s_copy(c, c_place(way, hop), piece).start()

    ring(lambda t: in_copy(1, t).wait_send())
    ring(lambda t: in_copy(2, t).wait_send())
    x_sent()
    for i in range(1, side):
        w_copy((place(c) + i) % side).wait_send()
        for o in range(2):
            for s in range(slots):
                for q in range(side if o == 0 else 1):
                    p_copy(s, o, (place(o) + i) % side, q).wait_send()
        for p in (2, 3):
            g_copy(p, (place(c) + i) % side).wait_send()

    def r_sent(n, carry):
        o = n % 2
        for kind in range(2):
            for i in range(1, side):
                r_copy(kind, o, n // 2, (place(1 - o) + i) % side).wait_send()
        return carry

    lax.fori_loop(0, 2 * steps, r_sent, 0)
    for k in range(side):
        f_copy(k).wait_send()

    t_copy().wait_send()
    for p in (2, 3):
        up_targets(lambda o, k, p=p: u_copy(o, p, k).wait_send())

    def q_sent(i, carry):
        q_copy((me + i) % n_t).wait_send()
        return carry

    lax.fori_loop(1, n_t, q_sent, 0)
    for p in range(4):
        z_part(p, lambda k, p=p: z_copy(p, k, z).wait_send())
    for way in range(2):
        for hop in range(reach[way]):
            for piece in range(2):
                c_copy(way, hop, piece).wait_send()
    for at in range(n_z):
        for piece in range(2):
            s_copy(c, at, piece).wait_send()
            s_copy(1 - c, at, piece).wait_recv()
    for which in range(2):
        for p in range(4):
            grad_out[which, :, starts[p] : starts[p] + sizes[p]] = final[p % 2][which, p // 2]


def on_device(n_t, n_dp, qkv_img, tan_img, txt_kv, head_table, out_weight, cotangent):
    rows, width = qkv_img.shape[1], qkv_img.shape[3]
    slots = head_table.shape[1]
    side = 4
    n_z = n_dp // 2
    txt_len = txt_kv.shape[2]
    img = n_t * rows
    keys = img + txt_len
    keys_pad = -(-keys // 128) * 128
    half = -(-width // 256) * 128
    offset = width - half
    dims = (n_t, side, n_z, slots, rows, keys, keys_pad, half, offset, width, txt_len)
    dma = pltpu.SemaphoreType.DMA
    vmem = pl.BlockSpec(memory_space=pltpu.VMEM)
    hbm = pl.BlockSpec(memory_space=pl.ANY)

    def both(*shape):
        return [pltpu.VMEM(shape + (384,), LOW), pltpu.VMEM(shape + (256,), LOW)]

    image, tangent, grad = pl.pallas_call(
        functools.partial(body, dims),
        out_shape=(
            jax.ShapeDtypeStruct((rows, width), LOW),
            jax.ShapeDtypeStruct((rows, width), LOW),
            jax.ShapeDtypeStruct((2, 192, half), LOW),
        ),
        in_specs=[pl.BlockSpec(memory_space=pltpu.SMEM)] + [hbm] * 5,
        out_specs=(vmem, vmem, vmem),
        scratch_shapes=[
            pltpu.VMEM((rows, width), LOW),
            pltpu.VMEM((3, rows, width), LOW),
            pltpu.VMEM((3, rows, width), LOW),
            pltpu.VMEM((slots, txt_len, 256), LOW),
            pltpu.VMEM((6, width // 128, rows, 128), LOW),
            pltpu.VMEM((slots, n_t, rows, 384), LOW),
            pltpu.VMEM((slots, n_t, rows, 384), LOW),
            pltpu.VMEM((384, 256), LOW),
            pltpu.VMEM((slots, 128, 2 * keys_pad), LOW),
            pltpu.VMEM((slots, 2 * keys_pad, 128), LOW),
            pltpu.VMEM((slots, side, side, rows, 128), LOW),
            pltpu.VMEM((2, slots, side, side, rows, 128), LOW),
            pltpu.VMEM((2, side * 256, half), LOW),
            pltpu.VMEM((2, 2, side * rows, side * 256), LOW),
            pltpu.VMEM((2, side, 192, side * rows), LOW),
            pltpu.VMEM((2, 2, 2, side, rows, half // 2), LOW),
            pltpu.VMEM((2, 2, 2, side, rows, half // 2), LOW),
            pltpu.VMEM((rows, width), F32),
            pltpu.VMEM((n_t, 8, 128), F32),
            *both(2, 2, rows),
            *both(2, 2, side * rows),
            pltpu.VMEM((side, 192, side * rows), LOW),
            *both(2, side, 192),
            *both(2, side, 192),
            *both(2, 192),
            *both(n_z, 2 * 192 // n_z),
            *both(2, 2, 192),
            dma((slots, n_t)),
            dma((slots, n_t)),
            dma((side,)),
            dma((side,)),
            dma((side, 2, n_z // 2)),
            dma((side, n_z)),
            dma((side,)),
            dma((side,)),
            dma((9 + slots,)),
            dma((2, slots, side, side)),
            dma((2, slots, side, side)),
            dma((2, 2, 2, side)),
            dma((2, 2, 2, side)),
            dma((n_t,)),
            dma((n_t,)),
            dma((2, 4, side)),
            dma((2, 4, side)),
            dma,
            dma,
            dma((4, side)),
            dma((4, side)),
            dma((4, n_z)),
            dma((2, n_z)),
            dma((2, n_z // 2, 2)),
            dma((n_z, 2)),
            dma((n_z, 2)),
            dma((n_z, 2)),
        ],
        compiler_params=pltpu.CompilerParams(
            collective_id=0, has_side_effects=True, vmem_limit_bytes=56 * 1024 * 1024
        ),
    )(
        head_table.T,
        jnp.transpose(qkv_img[0], (1, 0, 2)),
        jnp.transpose(tan_img[0], (1, 0, 2)),
        txt_kv[0],
        out_weight,
        cotangent[0],
    )
    return pl.pallas_call(
        finish,
        out_shape=(
            jax.ShapeDtypeStruct((rows, width), LOW),
            jax.ShapeDtypeStruct((rows, width), LOW),
            jax.ShapeDtypeStruct((slots * 64, width), F32),
        ),
        in_specs=[hbm, hbm, hbm],
        out_specs=(hbm, hbm, hbm),
        scratch_shapes=[
            pltpu.VMEM((2, rows, width), LOW),
            pltpu.VMEM((2, 192, half), LOW),
            pltpu.VMEM((192, width), F32),
            dma((4,)),
            dma((4,)),
            dma((4,)),
        ],
    )(image, tangent, grad)


def solution(mesh):
    n_t, n_dp = mesh.shape["tensor"], mesh.shape["dp"]

    def step(*args):
        image_out, tangent_out, weight_grad = on_device(n_t, n_dp, *args)
        return image_out[None], tangent_out[None], weight_grad

    return jax.shard_map(
        step,
        mesh=mesh,
        in_specs=(
            P("dp", "tensor", None, None),
            P("dp", "tensor", None, None),
            P("dp", "tensor", None, None),
            P(),
            P("tensor", None),
            P("dp", "tensor", None),
        ),
        out_specs=(P("dp", "tensor", None), P("dp", "tensor", None), P("tensor", None)),
        check_vma=False,
    )
```
